32 devices in a mesh: dp: 8 (over y, x, core), tensor: 4 (over z).
Axes of the slice: x: 2, y: 2, z: 4, core: 2. Of those that a mesh axis runs over, the one named last changes fastest.
Arguments:
- tokens: bfloat16 [4096, 6144], P('dp', 'tensor'), may hold values from -6 to 6
- block_mask: int32 [16, 4, 4], P('dp'), may hold values from 0 to 1
- norm_gain: float32 [6144], replicated, may hold values from 0.25 to 1.75
- w_query: bfloat16 [6144, 3072], P('dp', 'tensor'), may hold values from -0.078125 to 0.078125
- w_key: bfloat16 [6144, 3072], P('dp', 'tensor'), may hold values from -0.078125 to 0.078125
- w_value: bfloat16 [6144, 3072], P('dp', 'tensor'), may hold values from -0.078125 to 0.078125
- query_gain: float32 [128], replicated, may hold values from 0.1 to 1.9
- key_gain: float32 [128], replicated, may hold values from 0.1 to 1.9
Outputs:
- attended: bfloat16 [4096, 3072], P('dp', 'tensor')
The draws below stay inside these ranges and needn't reach their ends.
All inputs are finite; a program needn't handle non-finite values.
Results may differ from the reference program's by a relative error of at most 0.0085.
Values may be sent and summed in bfloat16 or wider, within the bound.
No kernel may reach another device: no remote copies, remote signals or barrier semaphores. Data moves between devices by JAX's collectives and lax.ppermute only.
A program may use at most 192 MiB of HBM per device.

```python
import jax
import jax.numpy as jnp
from jax import lax

D = 6144
DH = 128
HEADS = 24
TPD = 256
BLOCK = 64
NBLK = 4
HD = 3072
DRAWS = 16
TOKENS = 4096


def place_ends(entries, key, least, top_value):
    spot = [jax.random.randint(jax.random.fold_in(key, axis), (), 0, length) for axis, length in enumerate(entries.shape)]
    longest = entries.shape.index(max(entries.shape))
    beside = spot[:longest] + [(spot[longest] + 1) % entries.shape[longest]] + spot[longest + 1:]
    return entries.at[tuple(spot)].set(least).at[tuple(beside)].set(top_value)


def steps_of(own_key, dims, cuts, smallest, high):
    level = 1.0
    for dim, blocks in cuts:
        heights = jax.random.uniform(jax.random.fold_in(jax.random.fold_in(own_key, 6), dim), (blocks,), jnp.float32, smallest / len(cuts), high / len(cuts))
        level = level * jnp.repeat(jnp.exp(heights), dims[dim] // blocks).reshape((-1,) + (1,) * (len(dims) - 1 - dim))
    return level


def gaussian(stream_key, extent, scale, most, shards=(), held_as=jnp.bfloat16):
    values = scale * jax.random.normal(stream_key, extent, jnp.float32)
    if shards:
        values = values * steps_of(stream_key, extent, shards, -0.22, 0.18)
    return jnp.clip(values, -most, most).astype(held_as)


def setup_inputs(seed: int = 0) -> dict:
    seeds = jax.random.split(jax.random.key(seed), 9)
    tokens = gaussian(seeds[0], (TOKENS, D), 1.0, 6.0, ((0, 8), (1, 4)))
    block_mask = place_ends(jax.random.randint(seeds[1], (DRAWS, NBLK, NBLK), 0, 2), jax.random.fold_in(seeds[1], 1), 0, 1).astype(jnp.int32)
    norm_gain = jnp.clip(1.0 + 0.15 * jax.random.normal(seeds[2], (D,), jnp.float32), 0.25, 1.75)
    w_query = gaussian(seeds[3], (D, HD), D ** -0.5, 0.078125, ((0, 8), (1, 4)))
    w_key = gaussian(seeds[4], (D, HD), D ** -0.5, 0.078125, ((0, 8), (1, 4)))
    w_value = gaussian(seeds[5], (D, HD), D ** -0.5, 0.078125, ((0, 8), (1, 4)))
    query_gain = jnp.clip(1.0 + 0.18 * jax.random.normal(seeds[6], (DH,), jnp.float32), 0.1, 1.9)
    key_gain = jnp.clip(1.0 + 0.18 * jax.random.normal(seeds[7], (DH,), jnp.float32), 0.1, 1.9)
    return dict(tokens=tokens, block_mask=block_mask, norm_gain=norm_gain, w_query=w_query, w_key=w_key, w_value=w_value, query_gain=query_gain, key_gain=key_gain)


EPS = 1e-06

def layer_norm(rows, gain):
    values = rows.astype(jnp.float32)
    mean = lax.optimization_barrier(jnp.mean(values, axis=-1, keepdims=True))
    mean_sq = lax.optimization_barrier(jnp.mean(values * values, axis=-1, keepdims=True))
    return (values - mean) * lax.rsqrt(mean_sq - mean * mean + EPS) * gain

def head_norm(values, gain):
    mean_sq = lax.optimization_barrier(jnp.mean(values * values, axis=-1, keepdims=True))
    return values * lax.rsqrt(mean_sq + EPS) * gain

def expand_mask(block_mask):
    blocks = block_mask.shape[-1]
    allowed = (block_mask > 0) | (jnp.arange(blocks)[:, None] == jnp.arange(blocks)[None, :])
    allowed = jnp.repeat(jnp.repeat(allowed, BLOCK, axis=-2), BLOCK, axis=-1)
    return allowed

def reference(tokens, block_mask, norm_gain, w_query, w_key, w_value, query_gain, key_gain):
    normed = layer_norm(tokens, norm_gain).astype(jnp.bfloat16)
    query = jnp.dot(normed, w_query, preferred_element_type=jnp.float32)
    key = jnp.dot(normed, w_key, preferred_element_type=jnp.float32)
    value = jnp.dot(normed, w_value, preferred_element_type=jnp.float32).astype(jnp.bfloat16)
    query_n = head_norm(query.reshape(DRAWS, TPD, HEADS, DH), query_gain).astype(jnp.bfloat16)
    key_n = head_norm(key.reshape(DRAWS, TPD, HEADS, DH), key_gain).astype(jnp.bfloat16)
    value = value.reshape(DRAWS, TPD, HEADS, DH)

    def one_draw(items):
        qd, kd, vd, md = items
        scores = jnp.einsum('qhe,khe->hqk', qd.astype(jnp.float32), kd.astype(jnp.float32)) / jnp.sqrt(jnp.float32(DH))
        allowed = expand_mask(md)
        scores = jnp.where(allowed[None], scores, jnp.float32(-1e+30))
        top = lax.optimization_barrier(jnp.max(scores, axis=-1, keepdims=True))
        weights = jnp.exp(scores - top)
        probs = (weights / lax.optimization_barrier(jnp.sum(weights, axis=-1, keepdims=True))).astype(jnp.bfloat16)
        out = jnp.einsum('hqk,khe->qhe', probs.astype(jnp.float32), vd.astype(jnp.float32))
        return out.astype(jnp.bfloat16).reshape(TPD, HD)
    result = lax.map(one_draw, (query_n, key_n, value, block_mask))
    return result.reshape(TOKENS, HD)
```

```python
import functools

import jax
import jax.numpy as jnp
from jax import lax
from jax.experimental import pallas as pl
from jax.experimental.pallas import tpu as pltpu
from jax.sharding import PartitionSpec as P

DH = 128
TPD = 256
BLOCK = 64


EPS = 1e-06


def layer_norm(rows, gain):
    values = rows.astype(jnp.float32)
    mean = jnp.mean(values, axis=-1, keepdims=True)
    mean_sq = jnp.mean(values * values, axis=-1, keepdims=True)
    return (values - mean) * lax.rsqrt(mean_sq - mean * mean + EPS) * gain


def head_norm(values, gain):
    mean_sq = jnp.mean(values * values, axis=-1, keepdims=True)
    return values * lax.rsqrt(mean_sq + EPS) * gain


def add_rows(normed, piece):
    return jnp.dot(normed, piece, preferred_element_type=jnp.float32)


def allowed_pairs(block_mask):
    blocks = block_mask.shape[-1]
    allowed = (block_mask > 0) | (jnp.arange(blocks)[:, None] == jnp.arange(blocks)[None, :])[None]
    return jnp.repeat(jnp.repeat(allowed, BLOCK, axis=1), BLOCK, axis=2)


def per_device(tokens, block_mask, norm_gain, w_query, w_key, w_value, query_gain, key_gain):
    whole = lax.all_gather(tokens, "tensor", axis=1, tiled=True)
    normed = layer_norm(whole, norm_gain).astype(jnp.bfloat16)

    def add_one(piece):
        return add_rows(normed, piece)

    query = add_one(lax.all_gather(w_query, "dp", axis=0, tiled=True))
    key = add_one(lax.all_gather(w_key, "dp", axis=0, tiled=True))
    value = add_one(lax.all_gather(w_value, "dp", axis=0, tiled=True))
    draws_here = tokens.shape[0] // TPD
    heads_here = w_query.shape[1] // DH
    query_n = head_norm(query.reshape(draws_here, TPD, heads_here, DH), query_gain).astype(
        jnp.bfloat16
    )
    key_n = head_norm(key.reshape(draws_here, TPD, heads_here, DH), key_gain).astype(jnp.bfloat16)
    value = value.astype(jnp.bfloat16).reshape(draws_here, TPD, heads_here, DH)
    allowed = allowed_pairs(block_mask)
    scores = jnp.einsum(
        "bqhe,bkhe->bhqk", query_n, key_n, preferred_element_type=jnp.float32
    ) / jnp.sqrt(jnp.float32(DH))
    scores = jnp.where(allowed[:, None], scores, jnp.float32(-1e30))
    top = jnp.max(scores, axis=-1, keepdims=True)
    weights = jnp.exp(scores - top)
    probs = (weights / jnp.sum(weights, axis=-1, keepdims=True)).astype(jnp.bfloat16)
    out = jnp.einsum("bhqk,bkhe->bqhe", probs, value, preferred_element_type=jnp.float32)
    return out.astype(jnp.bfloat16).reshape(tokens.shape[0], heads_here * DH)


CORE, X, Y = 1, 2, 4

PLACES = ((0, 1, 2, 3), (1, 0, 2, 3), (2, 3, 1, 0), (3, 2, 1, 0))


def arrival(z, place):
    return z - place if place <= z else 3 + place - z


def plan(z, chip):
    diagonal = chip ^ 3
    order = [place for place in PLACES[z] if place != diagonal] + [diagonal]
    pairs = [number for place in order for number in (PLACES[z].index(place), place ^ chip)]
    return pairs + list(PLACES[z]) + [arrival(z, place) for place in PLACES[z]]


PLAN = [[plan(z, chip) for chip in range(4)] for z in range(4)]
PLACE, ARRIVAL, CORE_AT = 8, 12, 16

HBM = pl.BlockSpec(memory_space=pltpu.HBM)
ANY = pl.BlockSpec(memory_space=pl.ANY)
VMEM = pl.BlockSpec(memory_space=pltpu.VMEM)
SMEM = pl.BlockSpec(memory_space=pltpu.SMEM)
FREE = pl.CostEstimate(flops=0, bytes_accessed=0, transcendentals=0)
PARAMS = pltpu.CompilerParams(vmem_limit_bytes=56 * 2**20)


def swap(array, bits):
    return lax.ppermute(array, "dp", [(i, i ^ bits) for i in range(8)])


def gate(arrays, others):
    return pl.pallas_call(
        lambda *refs: None,
        in_specs=[ANY] * (len(arrays) + len(others)),
        out_specs=[ANY] * len(arrays),
        out_shape=[jax.ShapeDtypeStruct(array.shape, array.dtype) for array in arrays],
        input_output_aliases={number: number for number in range(len(arrays))},
        compiler_params=PARAMS,
        cost_estimate=FREE,
    )(*arrays, *others)


def pack_kernel(plan_ref, *refs):
    weights, outs, held, packed, in_sems, out_sems = refs[:3], refs[3:5], refs[5], refs[6], refs[7], refs[8]
    core = plan_ref[CORE_AT]
    _, heads, _, _ = packed.shape
    width = heads * DH

    def load(number, kind):
        first = pl.multiple_of((core if number == 0 else 1 - core) * width, DH)
        return pltpu.make_async_copy(
            weights[kind].at[:, pl.ds(first, width)], held.at[number, kind], in_sems.at[number, kind]
        )

    def store(number, h):
        return pltpu.make_async_copy(packed.at[number, h], outs[number].at[h], out_sems.at[number, h])

    for number in range(2):
        for kind in range(3):
            load(number, kind).start()
    for number in range(2):
        for kind in range(3):
            load(number, kind).wait()
        for h in range(heads):
            for kind in range(3):
                packed[number, h, :, kind * DH : (kind + 1) * DH] = held[
                    number, kind, :, h * DH : (h + 1) * DH
                ]
            store(number, h).start()
    for number in range(2):
        for h in range(heads):
            store(number, h).wait()


def pack(plan_here, *weights):
    rows, columns = weights[0].shape
    heads = columns // (2 * DH)
    packed = jax.ShapeDtypeStruct((heads, rows, 3 * DH), jnp.bfloat16)
    return pl.pallas_call(
        pack_kernel,
        in_specs=[SMEM] + [HBM] * 3,
        out_specs=[HBM] * 2,
        out_shape=[packed] * 2,
        scratch_shapes=[
            pltpu.VMEM((2, 3, rows, heads * DH), jnp.bfloat16),
            pltpu.VMEM((2, heads, rows, 3 * DH), jnp.bfloat16),
            pltpu.SemaphoreType.DMA((2, 3)),
            pltpu.SemaphoreType.DMA((2, heads)),
        ],
        compiler_params=PARAMS,
        cost_estimate=FREE,
    )(plan_here, *weights)


def fetch(chosen, choices, target, sem):
    for number, choice in choices.items():

        @pl.when(chosen == number)
        def _():
            pltpu.make_async_copy(choice, target, sem).start()


def norm_kernel(slots, numbers, plan_ref, mean_ref, scale_ref, gains_ref, *refs):
    arrays = dict(zip(numbers, refs))
    outs, (raw, normed, in_sems, out_sems) = refs[-4 - len(slots) : -4], refs[-4:]
    rows = raw.shape[1]
    step = 64
    for n, slot in enumerate(slots):
        fetch(plan_ref[ARRIVAL + slot], arrays, raw.at[n], in_sems.at[n])
    for n, slot in enumerate(slots):
        pltpu.make_async_copy(refs[0], raw.at[n], in_sems.at[n]).wait()
        gain = gains_ref[pl.ds(plan_ref[PLACE + slot], 1), :]

        @pl.loop(0, rows // step)
        def _(tile):
            at = pl.ds(pl.multiple_of(tile * step, step), step)
            values = raw[n, at, :].astype(jnp.float32)
            normed[n, at, :] = ((values - mean_ref[at, :]) * scale_ref[at, :] * gain).astype(jnp.bfloat16)

        pltpu.make_async_copy(normed.at[n], outs[n], out_sems.at[n]).start()
    for n, slot in enumerate(slots):
        pltpu.make_async_copy(normed.at[n], outs[n], out_sems.at[n]).wait()


def norm(plan_here, slots, mean, scale, gains, arrays, *others):
    rows, features = next(iter(arrays.values())).shape
    shape = (len(slots), rows, features)
    return pl.pallas_call(
        functools.partial(norm_kernel, slots, tuple(arrays)),
        in_specs=[SMEM] + [VMEM] * 3 + [ANY] * (len(arrays) + len(others)),
        out_specs=[HBM] * len(slots),
        out_shape=[jax.ShapeDtypeStruct(shape[1:], jnp.bfloat16)] * len(slots),
        scratch_shapes=[
            pltpu.VMEM(shape, jnp.bfloat16),
            pltpu.VMEM(shape, jnp.bfloat16),
            pltpu.SemaphoreType.DMA((len(slots),)),
            pltpu.SemaphoreType.DMA((len(slots),)),
        ],
        compiler_params=PARAMS,
        cost_estimate=FREE,
    )(plan_here, mean, scale, gains, *arrays.values(), *others)


def project_kernel(count, first, size, has_acc, plan_ref, *refs):
    here, there = dict(enumerate(refs[:size])), dict(enumerate(refs[size : 2 * size]))
    same, cross = dict(enumerate(refs[2 * size : 2 * size + 3])), dict(enumerate(refs[2 * size + 3 : 2 * size + 6]))
    rest = refs[2 * size + 6 :]
    if has_acc:
        acc_in, rest = rest[0], rest[1:]
    acc_ref, tokens, weights, total, token_sems, weight_sems, acc_sems = rest
    core = plan_ref[CORE_AT]
    heads, depth, _ = same[0].shape
    rows = here[0].shape[0]

    def weight_copy(n, part, h):
        return pltpu.make_async_copy(same[0].at[h], weights.at[n, part, h], weight_sems.at[n, part, h])

    def token_copy(n, side):
        at = pl.ds(side * rows, rows)
        return pltpu.make_async_copy(here[0], tokens.at[n, at], token_sems.at[n, side])

    def store(h):
        return pltpu.make_async_copy(total.at[h], acc_ref.at[h], acc_sems.at[1, h])

    def load(h):
        return pltpu.make_async_copy(acc_in.at[h], total.at[h], acc_sems.at[0, h])

    for n in range(count):
        slot, bits = plan_ref[2 * (first + n)], plan_ref[2 * (first + n) + 1]
        for h in range(heads):
            for part, choices in enumerate((same, cross)):
                views = {number: choice.at[h] for number, choice in choices.items()}
                fetch(bits, views, weights.at[n, part, h], weight_sems.at[n, part, h])
            if h == 0:
                for side, choices in enumerate((here, there)):
                    fetch(slot, choices, tokens.at[n, pl.ds(side * rows, rows)], token_sems.at[n, side])
            if has_acc and n == 0:
                load(h).start()
    for n in range(count):
        for side in range(2):
            token_copy(n, side).wait()

        @pl.loop(0, heads)
        def _(h):
            update = None
            for part in range(2):
                weight_copy(n, part, h).wait()
                offset = pl.multiple_of((core if part == 0 else 1 - core) * depth, depth)
                product = jnp.dot(
                    tokens[n, :, pl.ds(offset, depth)],
                    weights[n, part, h],
                    preferred_element_type=jnp.float32,
                )
                update = product if update is None else update + product
            if has_acc and n == 0:
                load(h).wait()
            if has_acc or n > 0:
                update = update + total[h]
            total[h] = update
            if n == count - 1:
                store(h).start()

    for h in range(heads):
        store(h).wait()


def project(plan_here, count, first, here, there, same, cross, acc=None):
    heads, depth, width = same[0].shape
    rows, features = here[0].shape
    operands = [*here, *there, *same, *cross] + ([] if acc is None else [acc])
    return pl.pallas_call(
        functools.partial(project_kernel, count, first, len(here), acc is not None),
        in_specs=[SMEM] + [ANY] * len(operands),
        out_specs=HBM,
        out_shape=jax.ShapeDtypeStruct((heads, 2 * rows, width), jnp.float32),
        scratch_shapes=[
            pltpu.VMEM((count, 2 * rows, features), jnp.bfloat16),
            pltpu.VMEM((count, 2, heads, depth, width), jnp.bfloat16),
            pltpu.VMEM((heads, 2 * rows, width), jnp.float32),
            pltpu.SemaphoreType.DMA((count, 2)),
            pltpu.SemaphoreType.DMA((count, 2, heads)),
            pltpu.SemaphoreType.DMA((2, heads)),
        ],
        compiler_params=PARAMS,
        cost_estimate=FREE,
    )(plan_here, *operands)


def attend(query, key, value, mask_ref, draw):
    scores = lax.dot_general(
        query, key, (((1,), (1,)), ((), ())), preferred_element_type=jnp.float32
    ) / jnp.sqrt(jnp.float32(DH))
    blocks = TPD // BLOCK
    column = lax.broadcasted_iota(jnp.int32, (1, TPD), 1) // BLOCK
    bands = []
    for i in range(blocks):
        allowed = column == i
        for j in range(blocks):
            allowed = allowed | ((column == j) & (mask_ref[(draw * blocks + i) * blocks + j] > 0))
        bands.append(
            jnp.where(allowed, scores[i * BLOCK : (i + 1) * BLOCK], jnp.float32(-1e30))
        )
    scores = jnp.concatenate(bands, axis=0)
    top = jnp.max(scores, axis=-1, keepdims=True)
    weights = jnp.exp(scores - top)
    probs = (weights / jnp.sum(weights, axis=-1, keepdims=True)).astype(jnp.bfloat16)
    return jnp.dot(probs, value, preferred_element_type=jnp.float32).astype(jnp.bfloat16)


def head_kernel(size, plan_ref, mask_ref, *refs):
    sides = dict(enumerate(refs[:size])), dict(enumerate(refs[size : 2 * size]))
    same, cross, acc, query_gain, key_gain, out_ref = refs[2 * size : 2 * size + 6]
    tokens, weights, total, out, token_sems, weight_sems, acc_sems, out_sems = refs[2 * size + 6 :]
    core = plan_ref[CORE_AT]
    heads, depth, _ = same.shape
    rows = sides[0][0].shape[0]

    def token_copy(side):
        return pltpu.make_async_copy(sides[0][0], tokens.at[side], token_sems.at[side])

    def weight_copy(part, h):
        return pltpu.make_async_copy((same, cross)[part].at[h], weights.at[part, h], weight_sems.at[part, h])

    def acc_copy(side, h):
        return pltpu.make_async_copy(acc.at[h, pl.ds(side * rows, rows)], total.at[side, h], acc_sems.at[side, h])

    def out_copy(side, h):
        whose = core if side == 0 else 1 - core
        return pltpu.make_async_copy(out.at[side, h], out_ref.at[whose, h], out_sems.at[side, h])

    for h in range(heads):
        weight_copy(0, h).start()
        weight_copy(1, h).start()
        for side in range(2):
            if h == 0:
                fetch(plan_ref[6], sides[side], tokens.at[side], token_sems.at[side])
            acc_copy(side, h).start()
    for h in range(heads):
        weight_copy(0, h).wait()
        weight_copy(1, h).wait()
        for side in range(2):
            if h == 0:
                token_copy(side).wait()
            acc_copy(side, h).wait()
            sums = total[side, h]
            for part in range(2):
                offset = pl.multiple_of((core if part == 0 else 1 - core) * depth, depth)
                sums = sums + jnp.dot(
                    tokens[side, :, pl.ds(offset, depth)],
                    weights[part, h],
                    preferred_element_type=jnp.float32,
                )
            query = head_norm(sums[:, :DH], query_gain[...]).astype(jnp.bfloat16)
            key = head_norm(sums[:, DH : 2 * DH], key_gain[...]).astype(jnp.bfloat16)
            value = sums[:, 2 * DH :].astype(jnp.bfloat16)
            draws = rows // TPD
            for draw in range(draws):
                at = slice(draw * TPD, (draw + 1) * TPD)
                out[side, h, at, :] = attend(query[at], key[at], value[at], mask_ref, side * draws + draw)
            out_copy(side, h).start()
    for side in range(2):
        for h in range(heads):
            out_copy(side, h).wait()


def attend_heads(plan_here, mask, here, there, same, cross, acc, query_gain, key_gain):
    heads, depth, width = same.shape
    rows, features = here[0].shape
    return pl.pallas_call(
        functools.partial(head_kernel, len(here)),
        in_specs=[SMEM] * 2 + [ANY] * (2 * len(here) + 3) + [VMEM] * 2,
        out_specs=HBM,
        out_shape=jax.ShapeDtypeStruct((2, heads, rows, DH), jnp.bfloat16),
        scratch_shapes=[
            pltpu.VMEM((2, rows, features), jnp.bfloat16),
            pltpu.VMEM((2, heads, depth, width), jnp.bfloat16),
            pltpu.VMEM((2, heads, rows, width), jnp.float32),
            pltpu.VMEM((2, heads, rows, DH), jnp.bfloat16),
            pltpu.SemaphoreType.DMA((2,)),
            pltpu.SemaphoreType.DMA((2, heads)),
            pltpu.SemaphoreType.DMA((2, heads)),
            pltpu.SemaphoreType.DMA((2, heads)),
        ],
        compiler_params=PARAMS,
        cost_estimate=FREE,
    )(plan_here, mask, *here, *there, same, cross, acc, query_gain, key_gain)


def per_device_8x4(tokens, block_mask, norm_gain, w_query, w_key, w_value, query_gain, key_gain):
    features = tokens.shape[1]
    heads = w_query.shape[1] // (2 * DH)
    dp, z = lax.axis_index("dp"), lax.axis_index("tensor")
    core = (dp % 2).astype(jnp.int32)
    plan_here = jnp.asarray(PLAN, jnp.int32)[z, dp // 2]
    plan_here = jnp.concatenate([plan_here, core[None]])

    def up(array, first):
        return lax.ppermute(array, "tensor", [(i, i + 1) for i in range(first, 3)])

    def down(array, last):
        return lax.ppermute(array, "tensor", [(i + 1, i) for i in range(last)])

    values = tokens.astype(jnp.float32)
    stats = jnp.stack([jnp.sum(values, axis=1), jnp.sum(values * values, axis=1)])
    mine, other = pack(plan_here, w_query, w_key, w_value)

    x_same, y_cross = swap(mine, X), swap(other, Y | CORE)
    up1, down1 = up(tokens, 0), down(tokens, 3)
    (stats,) = gate((stats,), ())
    stats = stats + lax.ppermute(stats, "tensor", [(i, i ^ 1) for i in range(4)])
    mask = block_mask.astype(jnp.float32).reshape(-1)
    mask = jnp.concatenate([mask, swap(mask, CORE)])

    mine, other = gate((mine, other), (x_same, y_cross, mask))
    x_cross, y_same = swap(other, X | CORE), swap(mine, Y)
    own_cross = swap(other, CORE)
    stats = stats + lax.ppermute(stats, "tensor", [(i, i ^ 2) for i in range(4)])
    up1, down1 = gate((up1, down1), (stats,))
    up2, down2 = up(up1, 1), down(down1, 2)

    total = stats / (4 * features)
    mean = total[0][:, None]
    scale = lax.rsqrt(total[1] - total[0] * total[0] + EPS)[:, None]
    gains = norm_gain.reshape(4, features)
    arrived = {0: tokens, 1: up1, 4: down1}
    here = list(norm(plan_here, (0, 1), mean, scale, gains, arrived))
    there = [swap(chunk, CORE) for chunk in here]

    x_same, y_cross = gate(
        (x_same, y_cross), (x_cross, y_same, own_cross)
    )
    diag_same, diag_cross = swap(x_same, Y), swap(y_cross, X)
    up3, down3 = up(up2, 2), down(down2, 1)
    arrived = {1: up1, 2: up2, 4: down1, 5: down2}
    here += norm(plan_here, (2,), mean, scale, gains, arrived)
    there.append(swap(here[2], CORE))
    same, cross = [mine, x_same, y_same], [own_cross, x_cross, y_cross]
    acc = project(plan_here, 2, 0, here, there, same, cross)

    arrived = {2: up2, 3: up3, 5: down2, 6: down3}
    here += norm(plan_here, (3,), mean, scale, gains, arrived, acc)
    there.append(swap(here[3], CORE))
    acc = project(plan_here, 1, 2, here, there, same, cross, acc)

    out = attend_heads(
        plan_here, mask, here, there, diag_same, diag_cross, acc, query_gain[None, :], key_gain[None, :]
    )
    out = lax.all_to_all(out, "dp", 0, 0, axis_index_groups=[[i, i + 1] for i in range(0, 8, 2)])
    return jnp.concatenate([out[i // heads, i % heads] for i in range(2 * heads)], axis=1)


def solution(mesh):
    eight_by_four = dict(mesh.shape) == {"dp": 8, "tensor": 4}
    return jax.shard_map(
        per_device_8x4 if eight_by_four else per_device,
        mesh=mesh,
        in_specs=(
            P("dp", "tensor"),
            P("dp", None, None),
            P(),
            P("dp", "tensor"),
            P("dp", "tensor"),
            P("dp", "tensor"),
            P(),
            P(),
        ),
        out_specs=P("dp", "tensor"),
        check_vma=False,
    )
```

```python
import functools

import jax
import jax.numpy as jnp
from jax import lax
from jax.experimental import pallas as pl
from jax.experimental.pallas import tpu as pltpu
from jax.sharding import PartitionSpec as P

DH = 128
TPD = 256
BLOCK = 64


EPS = 1e-06


def layer_norm(rows, gain):
    values = rows.astype(jnp.float32)
    mean = jnp.mean(values, axis=-1, keepdims=True)
    mean_sq = jnp.mean(values * values, axis=-1, keepdims=True)
    return (values - mean) * lax.rsqrt(mean_sq - mean * mean + EPS) * gain


def head_norm(values, gain):
    mean_sq = jnp.mean(values * values, axis=-1, keepdims=True)
    return values * lax.rsqrt(mean_sq + EPS) * gain


def add_rows(normed, piece):
    return jnp.dot(normed, piece, preferred_element_type=jnp.float32)


def allowed_pairs(block_mask):
    blocks = block_mask.shape[-1]
    allowed = (block_mask > 0) | (jnp.arange(blocks)[:, None] == jnp.arange(blocks)[None, :])[None]
    return jnp.repeat(jnp.repeat(allowed, BLOCK, axis=1), BLOCK, axis=2)


def per_device(tokens, block_mask, norm_gain, w_query, w_key, w_value, query_gain, key_gain):
    whole = lax.all_gather(tokens, "tensor", axis=1, tiled=True)
    normed = layer_norm(whole, norm_gain).astype(jnp.bfloat16)

    def add_one(piece):
        return add_rows(normed, piece)

    query = add_one(lax.all_gather(w_query, "dp", axis=0, tiled=True))
    key = add_one(lax.all_gather(w_key, "dp", axis=0, tiled=True))
    value = add_one(lax.all_gather(w_value, "dp", axis=0, tiled=True))
    draws_here = tokens.shape[0] // TPD
    heads_here = w_query.shape[1] // DH
    query_n = head_norm(query.reshape(draws_here, TPD, heads_here, DH), query_gain).astype(
        jnp.bfloat16
    )
    key_n = head_norm(key.reshape(draws_here, TPD, heads_here, DH), key_gain).astype(jnp.bfloat16)
    value = value.astype(jnp.bfloat16).reshape(draws_here, TPD, heads_here, DH)
    allowed = allowed_pairs(block_mask)
    scores = jnp.einsum(
        "bqhe,bkhe->bhqk", query_n, key_n, preferred_element_type=jnp.float32
    ) / jnp.sqrt(jnp.float32(DH))
    scores = jnp.where(allowed[:, None], scores, jnp.float32(-1e30))
    top = jnp.max(scores, axis=-1, keepdims=True)
    weights = jnp.exp(scores - top)
    probs = (weights / jnp.sum(weights, axis=-1, keepdims=True)).astype(jnp.bfloat16)
    out = jnp.einsum("bhqk,bkhe->bqhe", probs, value, preferred_element_type=jnp.float32)
    return out.astype(jnp.bfloat16).reshape(tokens.shape[0], heads_here * DH)


CORE, X, Y = 1, 2, 4

PLACES = ((0, 1, 2, 3), (1, 0, 2, 3), (2, 3, 1, 0), (3, 2, 1, 0))


def arrival(z, place):
    return z - place if place <= z else 3 + place - z


def plan(z, chip):
    diagonal = chip ^ 3
    order = [place for place in PLACES[z] if place != diagonal] + [diagonal]
    pairs = [number for place in order for number in (PLACES[z].index(place), place ^ chip)]
    return pairs + list(PLACES[z]) + [arrival(z, place) for place in PLACES[z]]


PLAN = [[plan(z, chip) for chip in range(4)] for z in range(4)]
PLACE, ARRIVAL, CORE_AT = 8, 12, 16

HBM = pl.BlockSpec(memory_space=pltpu.HBM)
ANY = pl.BlockSpec(memory_space=pl.ANY)
VMEM = pl.BlockSpec(memory_space=pltpu.VMEM)
SMEM = pl.BlockSpec(memory_space=pltpu.SMEM)
FREE = pl.CostEstimate(flops=0, bytes_accessed=0, transcendentals=0)


def params(mib):
    return pltpu.CompilerParams(vmem_limit_bytes=mib * 2**20)


def swap(array, bits):
    return lax.ppermute(array, "dp", [(i, i ^ bits) for i in range(8)])


def trade(array):
    return lax.all_to_all(array, "dp", 0, 0, axis_index_groups=[[i, i + 1] for i in range(0, 8, 2)])


def gate(arrays, others):
    return pl.pallas_call(
        lambda *refs: None,
        in_specs=[ANY] * (len(arrays) + len(others)),
        out_specs=[ANY] * len(arrays),
        out_shape=[jax.ShapeDtypeStruct(array.shape, array.dtype) for array in arrays],
        input_output_aliases={number: number for number in range(len(arrays))},
        compiler_params=params(1),
        cost_estimate=FREE,
    )(*arrays, *others)


def columns_of(heads):
    query = [h * 2 * DH for h in range(heads)]
    value = [heads * 2 * DH + h * DH for h in range(heads)]
    return query, [first + DH for first in query], value


def column_groups(width):
    return [(first, min(first + 2 * DH, width)) for first in range(0, width, 2 * DH)]


def pack_kernel(*refs):
    weights, outs, (held, packed, in_sems, out_sems) = refs[:3], refs[3:5], refs[5:]
    core = lax.axis_index("dp") % 2
    _, _, _, width = held.shape
    heads = width // DH

    def load(number, kind):
        first = pl.multiple_of((core if number == 0 else 1 - core) * width, DH)
        return pltpu.make_async_copy(
            weights[kind].at[:, pl.ds(first, width)], held.at[number, kind], in_sems.at[number, kind]
        )

    def store(number):
        return pltpu.make_async_copy(packed.at[number], outs[number], out_sems.at[number])

    for number in range(2):
        for kind in range(3):
            load(number, kind).start()
    for number in range(2):
        for kind, firsts in enumerate(columns_of(heads)):
            load(number, kind).wait()
            for h, first in enumerate(firsts):
                packed[number, :, first : first + DH] = held[number, kind, :, h * DH : (h + 1) * DH]
        store(number).start()
    for number in range(2):
        store(number).wait()


def pack(*weights):
    rows, columns = weights[0].shape
    shape = (rows, 3 * columns // 2)
    return pl.pallas_call(
        pack_kernel,
        in_specs=[HBM] * 3,
        out_specs=[HBM] * 2,
        out_shape=[jax.ShapeDtypeStruct(shape, jnp.bfloat16)] * 2,
        scratch_shapes=[
            pltpu.VMEM((2, 3, rows, columns // 2), jnp.bfloat16),
            pltpu.VMEM((2, *shape), jnp.bfloat16),
            pltpu.SemaphoreType.DMA((2, 3)),
            pltpu.SemaphoreType.DMA((2,)),
        ],
        compiler_params=params(56),
        cost_estimate=FREE,
    )(*weights)


def fetch(chosen, choices, target, sem):
    for number, choice in choices.items():

        @pl.when(chosen == number)
        def _():
            pltpu.make_async_copy(choice, target, sem).start()


def norm_kernel(slots, numbers, plan_ref, mean_ref, scale_ref, gains_ref, *refs):
    arrays = dict(zip(numbers, refs))
    out_ref, raw, normed, in_sems, out_sems = refs[-5:]
    rows = raw.shape[1]
    step = 64

    for n, slot in enumerate(slots):
        fetch(plan_ref[ARRIVAL + slot], arrays, raw.at[n], in_sems.at[n])
    for n, slot in enumerate(slots):
        gain = gains_ref[pl.ds(plan_ref[PLACE + slot], 1), :]
        pltpu.make_async_copy(refs[0], raw.at[n], in_sems.at[n]).wait()

        @pl.loop(0, rows // step)
        def _(tile):
            at = pl.ds(pl.multiple_of(tile * step, step), step)
            values = raw[n, at, :].astype(jnp.float32)
            normed[n, at, :] = ((values - mean_ref[at, :]) * scale_ref[at, :] * gain).astype(jnp.bfloat16)

        for copy in range(out_ref.shape[0]):
            pltpu.make_async_copy(normed.at[n], out_ref.at[copy, n], out_sems.at[copy, n]).start()
    for n in range(len(slots)):
        for copy in range(out_ref.shape[0]):
            pltpu.make_async_copy(normed.at[n], out_ref.at[copy, n], out_sems.at[copy, n]).wait()


def norm(plan_here, slots, copies, mean, scale, gains, arrays, *others):
    rows, features = next(iter(arrays.values())).shape
    shape = (len(slots), rows, features)
    return pl.pallas_call(
        functools.partial(norm_kernel, slots, tuple(arrays)),
        in_specs=[SMEM] + [VMEM] * 3 + [ANY] * len(arrays) + [ANY] * len(others),
        out_specs=HBM,
        out_shape=jax.ShapeDtypeStruct((copies, *shape), jnp.bfloat16),
        scratch_shapes=[
            pltpu.VMEM(shape, jnp.bfloat16),
            pltpu.VMEM(shape, jnp.bfloat16),
            pltpu.SemaphoreType.DMA((len(slots),)),
            pltpu.SemaphoreType.DMA((copies, len(slots))),
        ],
        compiler_params=params(16),
        cost_estimate=FREE,
    )(plan_here, mean, scale, gains, *arrays.values(), *others)


class Tokens:
    def __init__(self, arrays):
        self.arrays = arrays
        _, _, self.rows, self.features = self.arrays[0].shape
        self.tiles_here = self.rows // TPD
        self.count = 2 * self.tiles_here

    def tiles(self, core, refs):
        found = [{} for _ in range(self.count)]
        slot = 0
        for ref, array in zip(refs, self.arrays):
            for n in range(array.shape[1]):
                for tile, choices in enumerate(found):
                    whose = core if tile < self.tiles_here else 1 - core
                    choices[slot] = ref.at[whose, n, pl.ds(tile % self.tiles_here * TPD, TPD)]
                slot += 1
        return found, refs[len(self.arrays) :]


def weight_copies(core, pair, columns, target, sems):
    copies = []
    for part, source in enumerate(pair):
        depth = source.shape[0]
        first = pl.multiple_of((core if part == 0 else 1 - core) * depth, depth)
        at = pl.ds(columns[0], columns[1] - columns[0])
        copies.append(
            pltpu.make_async_copy(source.at[:, at], target.at[pl.ds(first, depth), at], sems.at[part])
        )
    return copies


def weight_group(core, chosen, choices, columns, target, sems):
    def start():
        for number, pair in choices.items():

            @pl.when(chosen == number)
            def _():
                for copy in weight_copies(core, pair, columns, target, sems):
                    copy.start()

    def wait():
        for copy in weight_copies(core, choices[0], columns, target, sems):
            copy.wait()

    return [(start, wait)]


def token_group(chosen, views, target, sem):
    return [(functools.partial(fetch, chosen, views, target, sem), pltpu.make_async_copy(views[0], target, sem).wait)]


def run(groups, steps, ahead):
    started = waited = 0
    for need, step in steps:
        while started < min(need + 1 + ahead, len(groups)):
            for start, _ in groups[started]:
                start()
            started += 1
        while waited <= need:
            for _, wait in groups[waited]:
                wait()
            waited += 1
        step()


def project_kernel(tokens_of, plan_ref, *refs):
    core = plan_ref[CORE_AT]
    tiles, refs = tokens_of.tiles(core, refs)
    choices = {0: (refs[0].at[core], refs[0].at[1 - core]), 1: (refs[1], refs[2]), 2: (refs[3], refs[4])}
    total, next_tokens, next_weights, tokens, weights, token_sems, weight_sems, next_sems = refs[5:]
    count, _, width = weights.shape
    cuts = [0, 2 * DH, 4 * DH, 6 * DH, width]

    def add(n, first, last, tile):
        update = jnp.dot(tokens[n, tile], weights[n, :, first:last], preferred_element_type=jnp.float32)
        if n > 0:
            update = update + total[tile, :, first:last]
        total[tile, :, first:last] = update

    groups, steps = [], []
    for n in range(count):
        slot, bits = plan_ref[2 * n], plan_ref[2 * n + 1]
        for piece, columns in enumerate(zip(cuts, cuts[1:])):
            group = weight_group(core, bits, choices, columns, weights.at[n], weight_sems.at[n, piece])
            if piece > 0:
                groups.append(group)
            for tile, views in enumerate(tiles):
                if piece == 0:
                    tile_group = token_group(slot, views, tokens.at[n, tile], token_sems.at[n, tile])
                    groups.append(group + tile_group if tile == 0 else tile_group)
                for first, last in column_groups(width):
                    if columns[0] <= first < columns[1]:
                        steps.append((len(groups) - 1, functools.partial(add, n, first, last, tile)))
    slot = jnp.where(plan_ref[4] == 3, plan_ref[6], plan_ref[4])
    for tile, views in enumerate(tiles):
        groups.append(token_group(slot, views, next_tokens.at[tile], token_sems.at[count, tile]))
    groups.append(weight_group(core, plan_ref[5], choices, (0, width), next_weights, next_sems))
    steps.append((len(groups) - 1, lambda: None))
    run(groups, steps, 5)


def project(plan_here, arrays, near):
    tokens = Tokens(arrays)
    depth, width = near[1].shape
    count = 2
    shape = (tokens.count, TPD, tokens.features)
    return pl.pallas_call(
        functools.partial(project_kernel, tokens),
        in_specs=[SMEM] + [HBM] * (len(arrays) + len(near)),
        out_specs=[VMEM] * 3,
        out_shape=[
            jax.ShapeDtypeStruct((tokens.count, TPD, width), jnp.float32),
            jax.ShapeDtypeStruct(shape, jnp.bfloat16),
            jax.ShapeDtypeStruct((tokens.features, width), jnp.bfloat16),
        ],
        scratch_shapes=[
            pltpu.VMEM((count, *shape), jnp.bfloat16),
            pltpu.VMEM((count, tokens.features, width), jnp.bfloat16),
            pltpu.SemaphoreType.DMA((count + 1, tokens.count)),
            pltpu.SemaphoreType.DMA((count, 4, 2)),
            pltpu.SemaphoreType.DMA((2,)),
        ],
        compiler_params=params(18),
        cost_estimate=FREE,
    )(plan_here, *arrays, *near)


def attend(query, key, value, mask_ref, draw):
    scores = lax.dot_general(
        query, key, (((1,), (1,)), ((), ())), preferred_element_type=jnp.float32
    )
    weights = jnp.exp(scores * (DH**-0.5))
    blocks = TPD // BLOCK
    column = lax.broadcasted_iota(jnp.int32, (1, TPD), 1) // BLOCK
    bands = []
    for i in range(blocks):
        allowed = column == i
        for j in range(blocks):
            allowed = allowed | ((column == j) & (mask_ref[(draw * blocks + i) * blocks + j] > 0))
        bands.append(jnp.where(allowed, weights[i * BLOCK : (i + 1) * BLOCK], 0.0))
    weights = jnp.concatenate(bands, axis=0).astype(jnp.bfloat16)
    both = jnp.dot(
        weights,
        jnp.concatenate([value, jnp.ones_like(value)], axis=1),
        preferred_element_type=jnp.float32,
    )
    return (both[:, :DH] / both[:, DH:]).astype(jnp.bfloat16)


def finish_kernel(
    plan_ref,
    mask_ref,
    total_ref,
    next_tokens,
    next_weights,
    last_here,
    last_there,
    diag_same,
    diag_cross,
    query_gain,
    key_gain,
    out_ref,
    near_tokens,
    diag_tokens,
):
    core = plan_ref[CORE_AT]
    tiles, _, width = total_ref.shape
    heads = width // (3 * DH)
    half = tiles // 2
    depth = diag_same.shape[0]

    def place(tile, near, diag):
        near_tokens[tile] = near(slice(None))
        for part in range(2):
            first = pl.multiple_of((core if part == 0 else 1 - core) * depth, depth)
            diag_tokens[part, tile] = diag(pl.ds(first, depth))

    for tile in range(tiles):
        at = pl.ds(tile % half * TPD, TPD)

        def last(features, at=at, ref=last_here if tile < half else last_there):
            return ref[0, 0, at, features]

        def early(features, tile=tile):
            return next_tokens[tile, :, features]

        @pl.when(plan_ref[4] == 3)
        def _():
            place(tile, last, early)

        @pl.when(plan_ref[4] != 3)
        def _():
            place(tile, early, last)

    query_first, key_first, value_first = columns_of(heads)
    for tile in range(tiles):
        sums = []
        for first, end in column_groups(width):
            part = total_ref[tile, :, first:end]
            for tokens, weights in (
                (near_tokens[tile], next_weights),
                (diag_tokens[0, tile], diag_same),
                (diag_tokens[1, tile], diag_cross),
            ):
                part = part + jnp.dot(tokens, weights[:, first:end], preferred_element_type=jnp.float32)
            sums += [part[:, at : at + DH] for at in range(0, end - first, DH)]
        whose = core if tile < half else 1 - core
        for h in range(heads):
            query = head_norm(sums[query_first[h] // DH], query_gain[...]).astype(jnp.bfloat16)
            key = head_norm(sums[key_first[h] // DH], key_gain[...]).astype(jnp.bfloat16)
            value = sums[value_first[h] // DH].astype(jnp.bfloat16)
            out_ref[whose, h, pl.ds(tile % half * TPD, TPD), :] = attend(
                query, key, value, mask_ref, whose * half + tile % half
            )


def finish(plan_here, mask, total, next_tokens, next_weights, last, diag, query_gain, key_gain):
    tiles, _, width = total.shape
    depth = diag[0].shape[0]
    heads = width // (3 * DH)
    return pl.pallas_call(
        finish_kernel,
        in_specs=[SMEM] * 2 + [VMEM] * 9,
        out_specs=VMEM,
        out_shape=jax.ShapeDtypeStruct((2, heads, tiles // 2 * TPD, DH), jnp.bfloat16),
        scratch_shapes=[
            pltpu.VMEM((tiles, TPD, 2 * depth), jnp.bfloat16),
            pltpu.VMEM((2, tiles, TPD, depth), jnp.bfloat16),
        ],
        compiler_params=params(18),
        cost_estimate=FREE,
    )(plan_here, mask, total, next_tokens, next_weights, *last, *diag, query_gain, key_gain)


def per_device_8x4(tokens, block_mask, norm_gain, w_query, w_key, w_value, query_gain, key_gain):
    features = tokens.shape[1]
    heads = w_query.shape[1] // (2 * DH)
    dp, z = lax.axis_index("dp"), lax.axis_index("tensor")
    core = (dp % 2).astype(jnp.int32)
    plan_here = jnp.asarray(PLAN, jnp.int32)[z, dp // 2]
    plan_here = jnp.concatenate([plan_here, core[None]])

    def up(array, first):
        return lax.ppermute(array, "tensor", [(i, i + 1) for i in range(first, 3)])

    def down(array, last):
        return lax.ppermute(array, "tensor", [(i + 1, i) for i in range(last)])

    mine, other = pack(w_query, w_key, w_value)
    values = tokens.astype(jnp.float32)
    stats = jnp.stack([jnp.sum(values, axis=1), jnp.sum(values * values, axis=1)])
    stats = stats + lax.ppermute(stats, "tensor", [(i, i ^ 1) for i in range(4)])

    x_same, y_cross = swap(mine, X), swap(other, Y | CORE)
    (sent,) = gate((tokens,), (stats, mine))
    up1, down1 = up(sent, 0), down(sent, 3)
    own = trade(jnp.where(core == 0, jnp.stack([mine, other]), jnp.stack([other, mine])))
    mask = block_mask.astype(jnp.float32).reshape(1, -1)
    mask = trade(jnp.concatenate([mask, mask])).reshape(-1)
    (stats,) = gate((stats,), (own, mask))
    stats = stats + lax.ppermute(stats, "tensor", [(i, i ^ 2) for i in range(4)])

    mine, other, up1, down1 = gate((mine, other, up1, down1), (x_same, y_cross, stats))
    x_cross, y_same = swap(other, X | CORE), swap(mine, Y)
    up2, down2 = up(up1, 1), down(down1, 2)

    means = stats / (4 * features)
    mean = means[0][:, None]
    scale = lax.rsqrt(means[1] - means[0] * means[0] + EPS)[:, None]
    gains = norm_gain.reshape(4, features)
    arrived = {0: tokens, 1: up1, 4: down1}
    normed = [trade(norm(plan_here, (0, 1), 2, mean, scale, gains, arrived))]

    x_same, y_cross, up2, down2 = gate(
        (x_same, y_cross, up2, down2), (x_cross, y_same, normed[0])
    )
    diag_same, diag_cross = swap(x_same, Y), swap(y_cross, X)
    up3, down3 = up(up2, 2), down(down2, 1)
    arrived = {1: up1, 2: up2, 4: down1, 5: down2}
    normed.append(trade(norm(plan_here, (2,), 2, mean, scale, gains, arrived)))
    near = [own, x_same, x_cross, y_same, y_cross]
    total, next_tokens, next_weights = project(plan_here, normed, near)

    arrived = {2: up2, 3: up3, 5: down2, 6: down3}
    last = norm(plan_here, (3,), 1, mean, scale, gains, arrived, total)
    last = (last, swap(last, CORE))
    out = finish(
        plan_here,
        mask,
        total,
        next_tokens,
        next_weights,
        last,
        (diag_same, diag_cross),
        query_gain[None, :],
        key_gain[None, :],
    )
    out = trade(out)
    return jnp.concatenate([out[i // heads, i % heads] for i in range(2 * heads)], axis=1)


def solution(mesh):
    eight_by_four = dict(mesh.shape) == {"dp": 8, "tensor": 4}
    return jax.shard_map(
        per_device_8x4 if eight_by_four else per_device,
        mesh=mesh,
        in_specs=(
            P("dp", "tensor"),
            P("dp", None, None),
            P(),
            P("dp", "tensor"),
            P("dp", "tensor"),
            P("dp", "tensor"),
            P(),
            P(),
        ),
        out_specs=P("dp", "tensor"),
        check_vma=False,
    )
```

```python
import functools

import jax
import jax.numpy as jnp
from jax import lax
from jax.experimental import pallas as pl
from jax.experimental.pallas import tpu as pltpu
from jax.sharding import PartitionSpec as P

DH = 128
TPD = 256
BLOCK = 64


EPS = 1e-06


def layer_norm(rows, gain):
    values = rows.astype(jnp.float32)
    mean = jnp.mean(values, axis=-1, keepdims=True)
    mean_sq = jnp.mean(values * values, axis=-1, keepdims=True)
    return (values - mean) * lax.rsqrt(mean_sq - mean * mean + EPS) * gain


def head_norm(values, gain):
    mean_sq = jnp.mean(values * values, axis=-1, keepdims=True)
    return values * lax.rsqrt(mean_sq + EPS) * gain


def add_rows(normed, piece):
    return jnp.dot(normed, piece, preferred_element_type=jnp.float32)


def allowed_pairs(block_mask):
    blocks = block_mask.shape[-1]
    allowed = (block_mask > 0) | (jnp.arange(blocks)[:, None] == jnp.arange(blocks)[None, :])[None]
    return jnp.repeat(jnp.repeat(allowed, BLOCK, axis=1), BLOCK, axis=2)


def per_device(tokens, block_mask, norm_gain, w_query, w_key, w_value, query_gain, key_gain):
    whole = lax.all_gather(tokens, "tensor", axis=1, tiled=True)
    normed = layer_norm(whole, norm_gain).astype(jnp.bfloat16)

    def add_one(piece):
        return add_rows(normed, piece)

    query = add_one(lax.all_gather(w_query, "dp", axis=0, tiled=True))
    key = add_one(lax.all_gather(w_key, "dp", axis=0, tiled=True))
    value = add_one(lax.all_gather(w_value, "dp", axis=0, tiled=True))
    draws_here = tokens.shape[0] // TPD
    heads_here = w_query.shape[1] // DH
    query_n = head_norm(query.reshape(draws_here, TPD, heads_here, DH), query_gain).astype(
        jnp.bfloat16
    )
    key_n = head_norm(key.reshape(draws_here, TPD, heads_here, DH), key_gain).astype(jnp.bfloat16)
    value = value.astype(jnp.bfloat16).reshape(draws_here, TPD, heads_here, DH)
    allowed = allowed_pairs(block_mask)
    scores = jnp.einsum(
        "bqhe,bkhe->bhqk", query_n, key_n, preferred_element_type=jnp.float32
    ) / jnp.sqrt(jnp.float32(DH))
    scores = jnp.where(allowed[:, None], scores, jnp.float32(-1e30))
    top = jnp.max(scores, axis=-1, keepdims=True)
    weights = jnp.exp(scores - top)
    probs = (weights / jnp.sum(weights, axis=-1, keepdims=True)).astype(jnp.bfloat16)
    out = jnp.einsum("bhqk,bkhe->bqhe", probs, value, preferred_element_type=jnp.float32)
    return out.astype(jnp.bfloat16).reshape(tokens.shape[0], heads_here * DH)


CORE, X, Y = 1, 2, 4

PLACES = ((0, 1, 2, 3), (1, 0, 2, 3), (2, 3, 1, 0), (3, 2, 1, 0))


def arrival(z, place):
    return z - place if place <= z else 3 + place - z


def plan(z, chip):
    diagonal = chip ^ 3
    order = [place for place in PLACES[z] if place != diagonal] + [diagonal]
    pairs = [number for place in order for number in (PLACES[z].index(place), place ^ chip)]
    return pairs + list(PLACES[z]) + [arrival(z, place) for place in PLACES[z]]


PLAN = [[plan(z, chip) for chip in range(4)] for z in range(4)]
PLACE, ARRIVAL, CORE_AT = 8, 12, 16

HBM = pl.BlockSpec(memory_space=pltpu.HBM)
ANY = pl.BlockSpec(memory_space=pl.ANY)
VMEM = pl.BlockSpec(memory_space=pltpu.VMEM)
SMEM = pl.BlockSpec(memory_space=pltpu.SMEM)
FREE = pl.CostEstimate(flops=0, bytes_accessed=0, transcendentals=0)


def params(mib):
    return pltpu.CompilerParams(vmem_limit_bytes=mib * 2**20)


def swap(array, bits):
    return lax.ppermute(array, "dp", [(i, i ^ bits) for i in range(8)])


def trade(array):
    return lax.all_to_all(array, "dp", 0, 0, axis_index_groups=[[i, i + 1] for i in range(0, 8, 2)])


def gate(arrays, others):
    return pl.pallas_call(
        lambda *refs: None,
        in_specs=[ANY] * (len(arrays) + len(others)),
        out_specs=[ANY] * len(arrays),
        out_shape=[jax.ShapeDtypeStruct(array.shape, array.dtype) for array in arrays],
        input_output_aliases={number: number for number in range(len(arrays))},
        compiler_params=params(1),
        cost_estimate=FREE,
    )(*arrays, *others)


def columns_of(heads):
    query = [h * 2 * DH for h in range(heads)]
    value = [heads * 2 * DH + h * DH for h in range(heads)]
    return query, [first + DH for first in query], value


def column_groups(width):
    return [(first, min(first + 2 * DH, width)) for first in range(0, width, 2 * DH)]


def pack_kernel(*refs):
    weights, outs, (held, packed, in_sems, out_sems) = refs[:3], refs[3:5], refs[5:]
    core = lax.axis_index("dp") % 2
    _, _, _, width = held.shape
    heads = width // DH

    def load(number, kind):
        first = pl.multiple_of((core if number == 0 else 1 - core) * width, DH)
        return pltpu.make_async_copy(
            weights[kind].at[:, pl.ds(first, width)], held.at[number, kind], in_sems.at[number, kind]
        )

    def store(number):
        return pltpu.make_async_copy(packed.at[number], outs[number], out_sems.at[number])

    for number in range(2):
        for kind in range(3):
            load(number, kind).start()
    for number in range(2):
        for kind, firsts in enumerate(columns_of(heads)):
            load(number, kind).wait()
            for h, first in enumerate(firsts):
                packed[number, :, first : first + DH] = held[number, kind, :, h * DH : (h + 1) * DH]
        store(number).start()
    for number in range(2):
        store(number).wait()


def pack(*weights):
    rows, columns = weights[0].shape
    shape = (rows, 3 * columns // 2)
    return pl.pallas_call(
        pack_kernel,
        in_specs=[HBM] * 3,
        out_specs=[HBM] * 2,
        out_shape=[jax.ShapeDtypeStruct(shape, jnp.bfloat16)] * 2,
        scratch_shapes=[
            pltpu.VMEM((2, 3, rows, columns // 2), jnp.bfloat16),
            pltpu.VMEM((2, *shape), jnp.bfloat16),
            pltpu.SemaphoreType.DMA((2, 3)),
            pltpu.SemaphoreType.DMA((2,)),
        ],
        compiler_params=params(56),
        cost_estimate=FREE,
    )(*weights)


def fetch(chosen, choices, target, sem):
    for number, choice in choices.items():

        @pl.when(chosen == number)
        def _():
            pltpu.make_async_copy(choice, target, sem).start()


def norm_kernel(slots, numbers, plan_ref, stats_ref, gains_ref, *refs):
    arrays = dict(zip(numbers, refs))
    out_ref, raw, normed, columns, in_sems, out_sems = refs[-6:]
    _, rows, features = raw.shape
    step = 64
    for n, slot in enumerate(slots):
        fetch(plan_ref[ARRIVAL + slot], arrays, raw.at[n], in_sems.at[n])
    stats = jnp.sum(stats_ref[...], axis=0) / (4 * features)
    mean = stats[0:1]
    scale = lax.rsqrt(stats[1:2] - mean * mean + EPS)
    columns[...] = jnp.concatenate([mean, scale, jnp.zeros((6, rows), jnp.float32)], axis=0).T
    for n, slot in enumerate(slots):
        gain = gains_ref[:, pl.ds(pl.multiple_of(plan_ref[PLACE + slot] * features, features), features)]
        pltpu.make_async_copy(refs[0], raw.at[n], in_sems.at[n]).wait()

        @pl.loop(0, rows // step)
        def _(tile):
            at = pl.ds(pl.multiple_of(tile * step, step), step)
            values = raw[n, at, :].astype(jnp.float32)
            normed[n, at, :] = ((values - columns[at, 0:1]) * columns[at, 1:2] * gain).astype(jnp.bfloat16)

        for copy in range(out_ref.shape[0]):
            pltpu.make_async_copy(normed.at[n], out_ref.at[copy, n], out_sems.at[copy, n]).start()
    for n in range(len(slots)):
        for copy in range(out_ref.shape[0]):
            pltpu.make_async_copy(normed.at[n], out_ref.at[copy, n], out_sems.at[copy, n]).wait()


def norm(plan_here, slots, copies, stats, gains, arrays, *others):
    rows, features = next(iter(arrays.values())).shape
    shape = (len(slots), rows, features)
    return pl.pallas_call(
        functools.partial(norm_kernel, slots, tuple(arrays)),
        in_specs=[SMEM] + [VMEM] * 2 + [ANY] * (len(arrays) + len(others)),
        out_specs=HBM,
        out_shape=jax.ShapeDtypeStruct((copies, *shape), jnp.bfloat16),
        scratch_shapes=[
            pltpu.VMEM(shape, jnp.bfloat16),
            pltpu.VMEM(shape, jnp.bfloat16),
            pltpu.VMEM((rows, 8), jnp.float32),
            pltpu.SemaphoreType.DMA((len(slots),)),
            pltpu.SemaphoreType.DMA((copies, len(slots))),
        ],
        compiler_params=params(16),
        cost_estimate=FREE,
    )(plan_here, stats, gains, *arrays.values(), *others)


class Tokens:
    def __init__(self, arrays):
        self.arrays = arrays
        _, _, self.rows, self.features = self.arrays[0].shape
        self.tiles_here = self.rows // TPD
        self.count = 2 * self.tiles_here

    def tiles(self, core, refs):
        found = [{} for _ in range(self.count)]
        slot = 0
        for ref, array in zip(refs, self.arrays):
            for n in range(array.shape[1]):
                for tile, choices in enumerate(found):
                    whose = core if tile < self.tiles_here else 1 - core
                    choices[slot] = ref.at[whose, n, pl.ds(tile % self.tiles_here * TPD, TPD)]
                slot += 1
        return found, refs[len(self.arrays) :]


def weight_copies(core, pair, columns, target, sems):
    copies = []
    for part, source in enumerate(pair):
        depth = source.shape[0]
        first = pl.multiple_of((core if part == 0 else 1 - core) * depth, depth)
        at = pl.ds(columns[0], columns[1] - columns[0])
        copies.append(
            pltpu.make_async_copy(source.at[:, at], target.at[pl.ds(first, depth), at], sems.at[part])
        )
    return copies


def weight_group(core, chosen, choices, columns, target, sems):
    def start():
        for number, pair in choices.items():

            @pl.when(chosen == number)
            def _():
                for copy in weight_copies(core, pair, columns, target, sems):
                    copy.start()

    def wait():
        for copy in weight_copies(core, choices[0], columns, target, sems):
            copy.wait()

    return [(start, wait)]


def token_group(chosen, views, target, sem):
    return [(functools.partial(fetch, chosen, views, target, sem), pltpu.make_async_copy(views[0], target, sem).wait)]


def run(groups, steps, ahead):
    started = waited = 0
    for need, step in steps:
        while started < min(need + 1 + ahead, len(groups)):
            for start, _ in groups[started]:
                start()
            started += 1
        while waited <= need:
            for _, wait in groups[waited]:
                wait()
            waited += 1
        step()


def project_kernel(tokens_of, plan_ref, *refs):
    core = plan_ref[CORE_AT]
    tiles, refs = tokens_of.tiles(core, refs)
    choices = {0: (refs[0].at[core], refs[0].at[1 - core]), 1: (refs[1], refs[2]), 2: (refs[3], refs[4])}
    total, next_tokens, next_weights, tokens, weights, token_sems, weight_sems, next_sems = refs[5:]
    count, _, width = weights.shape
    cuts = [0, 2 * DH, 4 * DH, 6 * DH, width]

    def add(n, first, last, tile):
        update = jnp.dot(tokens[n, tile], weights[n, :, first:last], preferred_element_type=jnp.float32)
        if n > 0:
            update = update + total[tile, :, first:last]
        total[tile, :, first:last] = update

    groups, steps = [], []
    for n in range(count):
        slot, bits = plan_ref[2 * n], plan_ref[2 * n + 1]
        for piece, columns in enumerate(zip(cuts, cuts[1:])):
            group = weight_group(core, bits, choices, columns, weights.at[n], weight_sems.at[n, piece])
            if piece > 0:
                groups.append(group)
            for tile, views in enumerate(tiles):
                if piece == 0:
                    tile_group = token_group(slot, views, tokens.at[n, tile], token_sems.at[n, tile])
                    groups.append(group + tile_group if tile == 0 else tile_group)
                for first, last in column_groups(width):
                    if columns[0] <= first < columns[1]:
                        steps.append((len(groups) - 1, functools.partial(add, n, first, last, tile)))
    slot = jnp.where(plan_ref[4] == 3, plan_ref[6], plan_ref[4])
    for tile, views in enumerate(tiles):
        groups.append(token_group(slot, views, next_tokens.at[tile], token_sems.at[count, tile]))
    groups.append(weight_group(core, plan_ref[5], choices, (0, width), next_weights, next_sems))
    steps.append((len(groups) - 1, lambda: None))
    run(groups, steps, 5)


def project(plan_here, arrays, near):
    tokens = Tokens(arrays)
    depth, width = near[1].shape
    count = 2
    shape = (tokens.count, TPD, tokens.features)
    return pl.pallas_call(
        functools.partial(project_kernel, tokens),
        in_specs=[SMEM] + [HBM] * (len(arrays) + len(near)),
        out_specs=[VMEM] * 3,
        out_shape=[
            jax.ShapeDtypeStruct((tokens.count, TPD, width), jnp.float32),
            jax.ShapeDtypeStruct(shape, jnp.bfloat16),
            jax.ShapeDtypeStruct((tokens.features, width), jnp.bfloat16),
        ],
        scratch_shapes=[
            pltpu.VMEM((count, *shape), jnp.bfloat16),
            pltpu.VMEM((count, tokens.features, width), jnp.bfloat16),
            pltpu.SemaphoreType.DMA((count + 1, tokens.count)),
            pltpu.SemaphoreType.DMA((count, 4, 2)),
            pltpu.SemaphoreType.DMA((2,)),
        ],
        compiler_params=params(18),
        cost_estimate=FREE,
    )(plan_here, *arrays, *near)


def attend(query, key, value, mask_ref, draw):
    scores = lax.dot_general(
        query, key, (((1,), (1,)), ((), ())), preferred_element_type=jnp.float32
    )
    weights = jnp.exp(scores * (DH**-0.5))
    blocks = TPD // BLOCK
    column = lax.broadcasted_iota(jnp.int32, (1, TPD), 1) // BLOCK
    bands = []
    for i in range(blocks):
        allowed = column == i
        for j in range(blocks):
            allowed = allowed | ((column == j) & (mask_ref[(draw * blocks + i) * blocks + j] > 0))
        bands.append(jnp.where(allowed, weights[i * BLOCK : (i + 1) * BLOCK], 0.0))
    weights = jnp.concatenate(bands, axis=0).astype(jnp.bfloat16)
    both = jnp.dot(
        weights,
        jnp.concatenate([value, jnp.ones_like(value)], axis=1),
        preferred_element_type=jnp.float32,
    )
    return (both[:, :DH] / both[:, DH:]).astype(jnp.bfloat16)


def finish_kernel(
    side,
    plan_ref,
    mask_ref,
    total_ref,
    next_tokens,
    next_weights,
    last_ref,
    diag_same,
    diag_cross,
    query_gain,
    key_gain,
    *refs,
):
    out_ref, near_tokens, diag_tokens = refs[-3:]
    core = plan_ref[CORE_AT]
    width = total_ref.shape[2]
    heads = width // (3 * DH)
    tiles = near_tokens.shape[0]
    depth = diag_same.shape[0]

    def place(tile, near, diag):
        near_tokens[tile] = near(slice(None))
        for part in range(2):
            first = pl.multiple_of((core if part == 0 else 1 - core) * depth, depth)
            diag_tokens[part, tile] = diag(pl.ds(first, depth))

    for tile in range(tiles):

        def last(features, tile=tile):
            return last_ref[0, 0, pl.ds(tile * TPD, TPD), features]

        def early(features, tile=tile):
            return next_tokens[side * tiles + tile, :, features]

        @pl.when(plan_ref[4] == 3)
        def _():
            place(tile, last, early)

        @pl.when(plan_ref[4] != 3)
        def _():
            place(tile, early, last)

    query_first, key_first, value_first = columns_of(heads)
    for tile in range(tiles):
        sums = []
        for first, end in column_groups(width):
            part = total_ref[side * tiles + tile, :, first:end]
            for tokens, weights in (
                (near_tokens[tile], next_weights),
                (diag_tokens[0, tile], diag_same),
                (diag_tokens[1, tile], diag_cross),
            ):
                part = part + jnp.dot(tokens, weights[:, first:end], preferred_element_type=jnp.float32)
            sums += [part[:, at : at + DH] for at in range(0, end - first, DH)]
        whose = core if side == 0 else 1 - core
        for h in range(heads):
            query = head_norm(sums[query_first[h] // DH], query_gain[...]).astype(jnp.bfloat16)
            key = head_norm(sums[key_first[h] // DH], key_gain[...]).astype(jnp.bfloat16)
            value = sums[value_first[h] // DH].astype(jnp.bfloat16)
            out_ref[pl.ds(tile * TPD, TPD), h * DH : (h + 1) * DH] = attend(
                query, key, value, mask_ref, whose * tiles + tile
            )


def finish(side, plan_here, mask, total, next_tokens, next_weights, last, diag, query_gain, key_gain, *others):
    tiles, _, width = total.shape
    depth = diag[0].shape[0]
    return pl.pallas_call(
        functools.partial(finish_kernel, side),
        in_specs=[SMEM] * 2 + [VMEM] * 8 + [ANY] * len(others),
        out_specs=VMEM,
        out_shape=jax.ShapeDtypeStruct((tiles // 2 * TPD, width // 3), jnp.bfloat16),
        scratch_shapes=[
            pltpu.VMEM((tiles // 2, TPD, 2 * depth), jnp.bfloat16),
            pltpu.VMEM((2, tiles // 2, TPD, depth), jnp.bfloat16),
        ],
        compiler_params=params(18),
        cost_estimate=FREE,
    )(plan_here, mask, total, next_tokens, next_weights, last, *diag, query_gain, key_gain, *others)


def per_device_8x4(tokens, block_mask, norm_gain, w_query, w_key, w_value, query_gain, key_gain):
    features = tokens.shape[1]
    heads = w_query.shape[1] // (2 * DH)
    dp, z = lax.axis_index("dp"), lax.axis_index("tensor")
    core = (dp % 2).astype(jnp.int32)
    plan_here = jnp.asarray(PLAN, jnp.int32)[z, dp // 2]
    plan_here = jnp.concatenate([plan_here, core[None]])

    def up(array, first):
        return lax.ppermute(array, "tensor", [(i, i + 1) for i in range(first, 3)])

    def down(array, last):
        return lax.ppermute(array, "tensor", [(i + 1, i) for i in range(last)])

    mine, other = pack(w_query, w_key, w_value)
    x_same, y_cross = swap(mine, X), swap(other, Y | CORE)
    up1, down1 = up(tokens, 0), down(tokens, 3)
    values = tokens.astype(jnp.float32)
    stats = jnp.stack([jnp.sum(values, axis=1), jnp.sum(values * values, axis=1)])
    own = trade(jnp.where(core == 0, jnp.stack([mine, other]), jnp.stack([other, mine])))
    mask = block_mask.astype(jnp.float32).reshape(1, -1)
    mask = trade(jnp.concatenate([mask, mask])).reshape(-1)
    (stats,) = gate((stats,), (own, mask))
    stats = lax.all_to_all(jnp.stack([stats] * 4), "tensor", 0, 0)
    gains = norm_gain.reshape(1, -1)

    mine, other, up1, down1, stats = gate((mine, other, up1, down1, stats), (x_same, y_cross))
    x_cross, y_same = swap(other, X | CORE), swap(mine, Y)
    up2, down2 = up(up1, 1), down(down1, 2)

    arrived = {0: tokens, 1: up1, 4: down1}
    normed = [trade(norm(plan_here, (0, 1), 2, stats, gains, arrived))]

    x_same, y_cross, up2, down2 = gate((x_same, y_cross, up2, down2), (x_cross, y_same, normed[0]))
    diag_same, diag_cross = swap(x_same, Y), swap(y_cross, X)
    up3, down3 = up(up2, 2), down(down2, 1)
    arrived = {1: up1, 2: up2, 4: down1, 5: down2}
    normed.append(trade(norm(plan_here, (2,), 2, stats, gains, arrived)))
    near = [own, x_same, x_cross, y_same, y_cross]
    total, next_tokens, next_weights = project(plan_here, normed, near)

    arrived = {2: up2, 3: up3, 5: down2, 6: down3}
    last = norm(plan_here, (3,), 1, stats, gains, arrived, total)
    diag = (diag_same, diag_cross)
    gain_pair = (query_gain[None, :], key_gain[None, :])
    early = (plan_here, mask, total, next_tokens, next_weights)
    theirs = finish(1, *early, swap(last, CORE), diag, *gain_pair)
    here = finish(0, *early, last, diag, *gain_pair, theirs)
    there = swap(theirs, CORE)
    return jnp.where(
        core == 0,
        jnp.concatenate([here, there], axis=1),
        jnp.concatenate([there, here], axis=1),
    )


def solution(mesh):
    eight_by_four = dict(mesh.shape) == {"dp": 8, "tensor": 4}
    return jax.shard_map(
        per_device_8x4 if eight_by_four else per_device,
        mesh=mesh,
        in_specs=(
            P("dp", "tensor"),
            P("dp", None, None),
            P(),
            P("dp", "tensor"),
            P("dp", "tensor"),
            P("dp", "tensor"),
            P(),
            P(),
        ),
        out_specs=P("dp", "tensor"),
        check_vma=False,
    )
```

```python
import functools

import jax
import jax.numpy as jnp
from jax import lax
from jax.experimental import pallas as pl
from jax.experimental.pallas import tpu as pltpu
from jax.sharding import PartitionSpec as P

DH = 128
TPD = 256
BLOCK = 64


EPS = 1e-06


def layer_norm(rows, gain):
    values = rows.astype(jnp.float32)
    mean = jnp.mean(values, axis=-1, keepdims=True)
    mean_sq = jnp.mean(values * values, axis=-1, keepdims=True)
    return (values - mean) * lax.rsqrt(mean_sq - mean * mean + EPS) * gain


def head_norm(values, gain):
    mean_sq = jnp.mean(values * values, axis=-1, keepdims=True)
    return values * lax.rsqrt(mean_sq + EPS) * gain


def add_rows(normed, piece):
    return jnp.dot(normed, piece, preferred_element_type=jnp.float32)


def allowed_pairs(block_mask):
    blocks = block_mask.shape[-1]
    allowed = (block_mask > 0) | (jnp.arange(blocks)[:, None] == jnp.arange(blocks)[None, :])[None]
    return jnp.repeat(jnp.repeat(allowed, BLOCK, axis=1), BLOCK, axis=2)


def per_device(tokens, block_mask, norm_gain, w_query, w_key, w_value, query_gain, key_gain):
    whole = lax.all_gather(tokens, "tensor", axis=1, tiled=True)
    normed = layer_norm(whole, norm_gain).astype(jnp.bfloat16)

    def add_one(piece):
        return add_rows(normed, piece)

    query = add_one(lax.all_gather(w_query, "dp", axis=0, tiled=True))
    key = add_one(lax.all_gather(w_key, "dp", axis=0, tiled=True))
    value = add_one(lax.all_gather(w_value, "dp", axis=0, tiled=True))
    draws_here = tokens.shape[0] // TPD
    heads_here = w_query.shape[1] // DH
    query_n = head_norm(query.reshape(draws_here, TPD, heads_here, DH), query_gain).astype(
        jnp.bfloat16
    )
    key_n = head_norm(key.reshape(draws_here, TPD, heads_here, DH), key_gain).astype(jnp.bfloat16)
    value = value.astype(jnp.bfloat16).reshape(draws_here, TPD, heads_here, DH)
    allowed = allowed_pairs(block_mask)
    scores = jnp.einsum(
        "bqhe,bkhe->bhqk", query_n, key_n, preferred_element_type=jnp.float32
    ) / jnp.sqrt(jnp.float32(DH))
    scores = jnp.where(allowed[:, None], scores, jnp.float32(-1e30))
    top = jnp.max(scores, axis=-1, keepdims=True)
    weights = jnp.exp(scores - top)
    probs = (weights / jnp.sum(weights, axis=-1, keepdims=True)).astype(jnp.bfloat16)
    out = jnp.einsum("bhqk,bkhe->bqhe", probs, value, preferred_element_type=jnp.float32)
    return out.astype(jnp.bfloat16).reshape(tokens.shape[0], heads_here * DH)


CORE, X, Y = 1, 2, 4

PLACES = ((0, 1, 2, 3), (1, 0, 2, 3), (2, 3, 1, 0), (3, 2, 1, 0))
OWN, PARTNER, MIDDLE, OUTWARD, MIDDLE_AGAIN, OUTWARD_AGAIN = range(6)
AT_ENDS = (OWN, PARTNER, OUTWARD, OUTWARD_AGAIN)
IN_MIDDLE = (OWN, PARTNER, MIDDLE, MIDDLE_AGAIN)
ARRIVALS = (AT_ENDS, IN_MIDDLE, IN_MIDDLE, AT_ENDS)
TO_PARTNER = ((0, 1), (1, 0), (2, 3), (3, 2))
TO_MIDDLE = ((1, 2), (2, 1))
TO_OUTSIDE = ((1, 0), (2, 3))


def plan(z, chip):
    diagonal = chip ^ 3
    order = [place for place in PLACES[z] if place != diagonal] + [diagonal]
    pairs = [number for place in order for number in (PLACES[z].index(place), place ^ chip)]
    return pairs + list(PLACES[z]) + list(ARRIVALS[z])


PLAN = [[plan(z, chip) for chip in range(4)] for z in range(4)]
PLACE, ARRIVAL, CORE_AT = 8, 12, 16

HBM = pl.BlockSpec(memory_space=pltpu.HBM)
ANY = pl.BlockSpec(memory_space=pl.ANY)
VMEM = pl.BlockSpec(memory_space=pltpu.VMEM)
SMEM = pl.BlockSpec(memory_space=pltpu.SMEM)
FREE = pl.CostEstimate(flops=0, bytes_accessed=0, transcendentals=0)


def params(mib):
    return pltpu.CompilerParams(vmem_limit_bytes=mib * 2**20)


def swap(array, bits):
    return lax.ppermute(array, "dp", [(i, i ^ bits) for i in range(8)])


def trade(array):
    return lax.all_to_all(array, "dp", 0, 0, axis_index_groups=[[i, i + 1] for i in range(0, 8, 2)])


def gate(arrays, others):
    return pl.pallas_call(
        lambda *refs: None,
        in_specs=[ANY] * (len(arrays) + len(others)),
        out_specs=[ANY] * len(arrays),
        out_shape=[jax.ShapeDtypeStruct(array.shape, array.dtype) for array in arrays],
        input_output_aliases={number: number for number in range(len(arrays))},
        compiler_params=params(1),
        cost_estimate=FREE,
    )(*arrays, *others)


def columns_of(heads):
    query = [h * 2 * DH for h in range(heads)]
    value = [heads * 2 * DH + h * DH for h in range(heads)]
    return query, [first + DH for first in query], value


def column_groups(width):
    return [(first, min(first + 2 * DH, width)) for first in range(0, width, 2 * DH)]


def pack_kernel(theirs, *refs):
    weights, out_ref, held, in_sems = refs[:3], *refs[-3:]
    core = lax.axis_index("dp") % 2
    width = held.shape[2]
    heads = width // DH

    def load(kind):
        first = pl.multiple_of((1 - core if theirs else core) * width, DH)
        return pltpu.make_async_copy(
            weights[kind].at[:, pl.ds(first, width)], held.at[kind], in_sems.at[kind]
        )

    for kind in range(3):
        load(kind).start()
    for kind, firsts in enumerate(columns_of(heads)):
        load(kind).wait()
        for h, first in enumerate(firsts):
            out_ref[:, first : first + DH] = held[kind, :, h * DH : (h + 1) * DH]


def pack(theirs, weights, *others):
    rows, columns = weights[0].shape
    return pl.pallas_call(
        functools.partial(pack_kernel, theirs),
        in_specs=[HBM] * 3 + [ANY] * len(others),
        out_specs=VMEM,
        out_shape=jax.ShapeDtypeStruct((rows, 3 * columns // 2), jnp.bfloat16),
        scratch_shapes=[
            pltpu.VMEM((3, rows, columns // 2), jnp.bfloat16),
            pltpu.SemaphoreType.DMA((3,)),
        ],
        compiler_params=params(56),
        cost_estimate=FREE,
    )(*weights, *others)


def fetch(chosen, choices, target, sem):
    for number, choice in choices.items():

        @pl.when(chosen == number)
        def _():
            pltpu.make_async_copy(choice, target, sem).start()


def norm_kernel(slots, numbers, plan_ref, stats_ref, gains_ref, *refs):
    arrays = dict(zip(numbers, refs))
    out_ref, raw, normed, columns, in_sems, out_sems = refs[-6:]
    _, rows, features = raw.shape
    step = 64
    for n, slot in enumerate(slots):
        fetch(plan_ref[ARRIVAL + slot], arrays, raw.at[n], in_sems.at[n])
    stats = jnp.sum(stats_ref[...], axis=0) / (4 * features)
    mean = stats[0:1]
    scale = lax.rsqrt(stats[1:2] - mean * mean + EPS)
    columns[...] = jnp.concatenate([mean, scale, jnp.zeros((6, rows), jnp.float32)], axis=0).T
    for n, slot in enumerate(slots):
        gain = gains_ref[:, pl.ds(pl.multiple_of(plan_ref[PLACE + slot] * features, features), features)]
        pltpu.make_async_copy(refs[0], raw.at[n], in_sems.at[n]).wait()

        @pl.loop(0, rows // step)
        def _(tile):
            at = pl.ds(pl.multiple_of(tile * step, step), step)
            values = raw[n, at, :].astype(jnp.float32)
            normed[n, at, :] = ((values - columns[at, 0:1]) * columns[at, 1:2] * gain).astype(jnp.bfloat16)

        for copy in range(out_ref.shape[0]):
            pltpu.make_async_copy(normed.at[n], out_ref.at[copy, n], out_sems.at[copy, n]).start()
    for n in range(len(slots)):
        for copy in range(out_ref.shape[0]):
            pltpu.make_async_copy(normed.at[n], out_ref.at[copy, n], out_sems.at[copy, n]).wait()


def norm(plan_here, slots, copies, stats, gains, arrays, *others):
    rows, features = next(iter(arrays.values())).shape
    shape = (len(slots), rows, features)
    return pl.pallas_call(
        functools.partial(norm_kernel, slots, tuple(arrays)),
        in_specs=[SMEM] + [VMEM] * 2 + [ANY] * (len(arrays) + len(others)),
        out_specs=HBM,
        out_shape=jax.ShapeDtypeStruct((copies, *shape), jnp.bfloat16),
        scratch_shapes=[
            pltpu.VMEM(shape, jnp.bfloat16),
            pltpu.VMEM(shape, jnp.bfloat16),
            pltpu.VMEM((rows, 8), jnp.float32),
            pltpu.SemaphoreType.DMA((len(slots),)),
            pltpu.SemaphoreType.DMA((copies, len(slots))),
        ],
        compiler_params=params(16),
        cost_estimate=FREE,
    )(plan_here, stats, gains, *arrays.values(), *others)


class Tokens:
    def __init__(self, arrays):
        self.arrays = arrays
        _, _, self.rows, self.features = self.arrays[0].shape
        self.tiles_here = self.rows // TPD
        self.count = 2 * self.tiles_here

    def tiles(self, core, refs):
        found = [{} for _ in range(self.count)]
        slot = 0
        for ref, array in zip(refs, self.arrays):
            for n in range(array.shape[1]):
                for tile, choices in enumerate(found):
                    whose = core if tile < self.tiles_here else 1 - core
                    choices[slot] = ref.at[whose, n, pl.ds(tile % self.tiles_here * TPD, TPD)]
                slot += 1
        return found, refs[len(self.arrays) :]


def weight_copies(core, pair, columns, target, sems):
    copies = []
    for part, source in enumerate(pair):
        depth = source.shape[0]
        first = pl.multiple_of((core if part == 0 else 1 - core) * depth, depth)
        at = pl.ds(columns[0], columns[1] - columns[0])
        copies.append(
            pltpu.make_async_copy(source.at[:, at], target.at[pl.ds(first, depth), at], sems.at[part])
        )
    return copies


def weight_group(core, chosen, choices, columns, target, sems):
    def start():
        for number, pair in choices.items():

            @pl.when(chosen == number)
            def _():
                for copy in weight_copies(core, pair, columns, target, sems):
                    copy.start()

    def wait():
        for copy in weight_copies(core, choices[0], columns, target, sems):
            copy.wait()

    return [(start, wait)]


def token_group(chosen, views, target, sem):
    return [(functools.partial(fetch, chosen, views, target, sem), pltpu.make_async_copy(views[0], target, sem).wait)]


def run(groups, steps, ahead):
    started = waited = 0
    for need, step in steps:
        while started < min(need + 1 + ahead, len(groups)):
            for start, _ in groups[started]:
                start()
            started += 1
        while waited <= need:
            for _, wait in groups[waited]:
                wait()
            waited += 1
        step()


def project_kernel(tokens_of, plan_ref, *refs):
    core = plan_ref[CORE_AT]
    tiles, refs = tokens_of.tiles(core, refs)
    choices = {0: (refs[0].at[core], refs[0].at[1 - core]), 1: (refs[1], refs[2]), 2: (refs[3], refs[4])}
    total, next_tokens, next_weights, tokens, weights, token_sems, weight_sems, next_sems = refs[5:]
    count, _, width = weights.shape
    cuts = [0, 2 * DH, 4 * DH, 6 * DH, width]

    def add(n, first, last, tile):
        update = jnp.dot(tokens[n, tile], weights[n, :, first:last], preferred_element_type=jnp.float32)
        if n > 0:
            update = update + total[tile, :, first:last]
        total[tile, :, first:last] = update

    groups, steps = [], []
    for n in range(count):
        slot, bits = plan_ref[2 * n], plan_ref[2 * n + 1]
        for piece, columns in enumerate(zip(cuts, cuts[1:])):
            group = weight_group(core, bits, choices, columns, weights.at[n], weight_sems.at[n, piece])
            if piece > 0:
                groups.append(group)
            for tile, views in enumerate(tiles):
                if piece == 0:
                    tile_group = token_group(slot, views, tokens.at[n, tile], token_sems.at[n, tile])
                    groups.append(group + tile_group if tile == 0 else tile_group)
                for first, last in column_groups(width):
                    if columns[0] <= first < columns[1]:
                        steps.append((len(groups) - 1, functools.partial(add, n, first, last, tile)))
    slot = jnp.where(plan_ref[4] == 3, plan_ref[6], plan_ref[4])
    for tile, views in enumerate(tiles):
        groups.append(token_group(slot, views, next_tokens.at[tile], token_sems.at[count, tile]))
    groups.append(weight_group(core, plan_ref[5], choices, (0, width), next_weights, next_sems))
    steps.append((len(groups) - 1, lambda: None))
    run(groups, steps, 5)


def project(plan_here, arrays, near):
    tokens = Tokens(arrays)
    depth, width = near[1].shape
    count = 2
    shape = (tokens.count, TPD, tokens.features)
    return pl.pallas_call(
        functools.partial(project_kernel, tokens),
        in_specs=[SMEM] + [HBM] * (len(arrays) + len(near)),
        out_specs=[VMEM] * 3,
        out_shape=[
            jax.ShapeDtypeStruct((tokens.count, TPD, width), jnp.float32),
            jax.ShapeDtypeStruct(shape, jnp.bfloat16),
            jax.ShapeDtypeStruct((tokens.features, width), jnp.bfloat16),
        ],
        scratch_shapes=[
            pltpu.VMEM((count, *shape), jnp.bfloat16),
            pltpu.VMEM((count, tokens.features, width), jnp.bfloat16),
            pltpu.SemaphoreType.DMA((count + 1, tokens.count)),
            pltpu.SemaphoreType.DMA((count, 4, 2)),
            pltpu.SemaphoreType.DMA((2,)),
        ],
        compiler_params=params(18),
        cost_estimate=FREE,
    )(plan_here, *arrays, *near)


def attend(query, key, value, mask_ref, draw):
    scores = lax.dot_general(
        query, key, (((1,), (1,)), ((), ())), preferred_element_type=jnp.float32
    )
    weights = jnp.exp(scores * (DH**-0.5))
    blocks = TPD // BLOCK
    column = lax.broadcasted_iota(jnp.int32, (1, TPD), 1) // BLOCK
    bands = []
    for i in range(blocks):
        allowed = column == i
        for j in range(blocks):
            allowed = allowed | ((column == j) & (mask_ref[(draw * blocks + i) * blocks + j] > 0))
        bands.append(jnp.where(allowed, weights[i * BLOCK : (i + 1) * BLOCK], 0.0))
    weights = jnp.concatenate(bands, axis=0).astype(jnp.bfloat16)
    both = jnp.dot(
        weights,
        jnp.concatenate([value, jnp.ones_like(value)], axis=1),
        preferred_element_type=jnp.float32,
    )
    return (both[:, :DH] / both[:, DH:]).astype(jnp.bfloat16)


def place(plan_ref, side, next_tokens, last_ref, near_tokens=None, diag_tokens=None):
    core = plan_ref[CORE_AT]
    tiles = last_ref.shape[2] // TPD

    def copy(near, diag):
        if near_tokens is not None:
            near_tokens[...] = near(slice(None))
        if diag_tokens is not None:
            depth = diag_tokens.shape[2]
            for part in range(2):
                first = pl.multiple_of((core if part == 0 else 1 - core) * depth, depth)
                diag_tokens[part] = diag(pl.ds(first, depth))

    def last(features):
        return last_ref[0, 0, :, features]

    def early(features):
        chunk = next_tokens[side * tiles : (side + 1) * tiles, :, features]
        return chunk.reshape(tiles * TPD, chunk.shape[2])

    @pl.when(plan_ref[4] == 3)
    def _():
        copy(last, early)

    @pl.when(plan_ref[4] != 3)
    def _():
        copy(early, last)


def near_kernel(side, plan_ref, total_ref, next_tokens, next_weights, last_ref, *refs):
    out_ref, near_tokens = refs[-2:]
    place(plan_ref, side, next_tokens, last_ref, near_tokens=near_tokens)
    tiles, _, width = out_ref.shape
    for tile in range(tiles):
        rows = near_tokens[tile * TPD : (tile + 1) * TPD, :]
        for first, end in column_groups(width):
            out_ref[tile, :, first:end] = total_ref[side * tiles + tile, :, first:end] + jnp.dot(
                rows, next_weights[:, first:end], preferred_element_type=jnp.float32
            )


def add_near(side, plan_here, total, next_tokens, next_weights, last):
    tiles, _, width = total.shape
    _, _, rows, features = last.shape
    return pl.pallas_call(
        functools.partial(near_kernel, side),
        in_specs=[SMEM] + [VMEM] * 4,
        out_specs=VMEM,
        out_shape=jax.ShapeDtypeStruct((tiles // 2, TPD, width), jnp.float32),
        scratch_shapes=[pltpu.VMEM((rows, features), jnp.bfloat16)],
        compiler_params=params(18),
        cost_estimate=FREE,
    )(plan_here, total, next_tokens, next_weights, last)


def finish_kernel(
    side,
    first_tile,
    plan_ref,
    mask_ref,
    total_ref,
    next_tokens,
    last_ref,
    diag_same,
    diag_cross,
    query_gain,
    key_gain,
    *refs,
):
    out_ref, near_tokens, diag_tokens = refs[-3:]
    core = plan_ref[CORE_AT]
    width = total_ref.shape[2]
    heads = width // (3 * DH)
    tiles = last_ref.shape[2] // TPD
    near = near_tokens.shape[0] > TPD
    place(plan_ref, side, next_tokens, last_ref, near_tokens if near else None, diag_tokens)
    query_first, key_first, value_first = columns_of(heads)
    for tile in range(tiles):
        sums = []
        at = slice(tile * TPD, (tile + 1) * TPD)
        pairs = [(diag_tokens[0, at], diag_same), (diag_tokens[1, at], diag_cross)]
        if near:
            pairs.append((near_tokens[at, :], refs[0]))
        for first, end in column_groups(width):
            part = total_ref[first_tile + tile, :, first:end]
            for tokens, weights in pairs:
                part = part + jnp.dot(tokens, weights[:, first:end], preferred_element_type=jnp.float32)
            sums += [part[:, column : column + DH] for column in range(0, end - first, DH)]
        whose = core if side == 0 else 1 - core
        for h in range(heads):
            query = head_norm(sums[query_first[h] // DH], query_gain[...]).astype(jnp.bfloat16)
            key = head_norm(sums[key_first[h] // DH], key_gain[...]).astype(jnp.bfloat16)
            value = sums[value_first[h] // DH].astype(jnp.bfloat16)
            out_ref[at, h * DH : (h + 1) * DH] = attend(query, key, value, mask_ref, whose * tiles + tile)


def finish(side, plan_here, mask, total, next_tokens, last, diag, gains, next_weights=None, others=()):
    width = total.shape[2]
    _, _, rows, features = last.shape
    near = next_weights is not None
    return pl.pallas_call(
        functools.partial(finish_kernel, side, side * rows // TPD if near else 0),
        in_specs=[SMEM] * 2 + [VMEM] * (8 if near else 7) + [ANY] * len(others),
        out_specs=VMEM,
        out_shape=jax.ShapeDtypeStruct((rows, width // 3), jnp.bfloat16),
        scratch_shapes=[
            pltpu.VMEM((rows if near else 16, features), jnp.bfloat16),
            pltpu.VMEM((2, rows, diag[0].shape[0]), jnp.bfloat16),
        ],
        compiler_params=params(18),
        cost_estimate=FREE,
    )(plan_here, mask, total, next_tokens, last, *diag, *gains, *([next_weights] if near else []), *others)


def per_device_8x4(tokens, block_mask, norm_gain, w_query, w_key, w_value, query_gain, key_gain):
    features = tokens.shape[1]
    heads = w_query.shape[1] // (2 * DH)
    dp, z = lax.axis_index("dp"), lax.axis_index("tensor")
    core = (dp % 2).astype(jnp.int32)
    plan_here = jnp.asarray(PLAN, jnp.int32)[z, dp // 2]
    plan_here = jnp.concatenate([plan_here, core[None]])

    def along(array, pairs):
        return lax.ppermute(array, "tensor", pairs)

    mine = pack(False, (w_query, w_key, w_value))
    x_same, y_same = swap(mine, X), swap(mine, Y)
    partner, middle = along(tokens, TO_PARTNER), along(tokens, TO_MIDDLE)
    values = tokens.astype(jnp.float32)
    stats = jnp.stack([jnp.sum(values, axis=1), jnp.sum(values * values, axis=1)])
    other = pack(True, (w_query, w_key, w_value), mine)
    own = trade(jnp.where(core == 0, jnp.stack([mine, other]), jnp.stack([other, mine])))
    mask = block_mask.astype(jnp.float32).reshape(1, -1)
    mask = trade(jnp.concatenate([mask, mask])).reshape(-1)
    (stats,) = gate((stats,), (own, mask))
    stats = lax.all_to_all(jnp.stack([stats] * 4), "tensor", 0, 0)
    gains = norm_gain.reshape(1, -1)

    other, partner, middle, stats = gate((other, partner, middle, stats), (x_same, y_same))
    x_cross, y_cross = swap(other, X | CORE), swap(other, Y | CORE)
    outward, middle_again = along(middle, TO_OUTSIDE), along(partner, TO_MIDDLE)

    arrived = {OWN: tokens, PARTNER: partner}
    normed = [trade(norm(plan_here, (0, 1), 2, stats, gains, arrived))]

    x_same, y_cross, outward, middle_again = gate(
        (x_same, y_cross, outward, middle_again), (x_cross, normed[0])
    )
    diag_same, diag_cross = swap(x_same, Y), swap(y_cross, X)
    outward_again = along(middle_again, TO_OUTSIDE)
    arrived = {MIDDLE: middle, OUTWARD: outward}
    normed.append(trade(norm(plan_here, (2,), 2, stats, gains, arrived)))
    near = [own, x_same, x_cross, y_same, y_cross]
    total, next_tokens, next_weights = project(plan_here, normed, near)

    arrived = {MIDDLE_AGAIN: middle_again, OUTWARD_AGAIN: outward_again}
    last = norm(plan_here, (3,), 1, stats, gains, arrived, total)
    diag = (diag_same, diag_cross)
    gain_pair = (query_gain[None, :], key_gain[None, :])
    last_there = swap(last, CORE)
    total_here = add_near(0, plan_here, total, next_tokens, next_weights, last)
    (last_there,) = gate((last_there,), (total_here,))
    theirs = finish(1, plan_here, mask, total, next_tokens, last_there, diag, gain_pair, next_weights)
    here = finish(0, plan_here, mask, total_here, next_tokens, last, diag, gain_pair, others=(theirs,))
    there = swap(theirs, CORE)
    return jnp.where(
        core == 0,
        jnp.concatenate([here, there], axis=1),
        jnp.concatenate([there, here], axis=1),
    )


def solution(mesh):
    eight_by_four = dict(mesh.shape) == {"dp": 8, "tensor": 4}
    return jax.shard_map(
        per_device_8x4 if eight_by_four else per_device,
        mesh=mesh,
        in_specs=(
            P("dp", "tensor"),
            P("dp", None, None),
            P(),
            P("dp", "tensor"),
            P("dp", "tensor"),
            P("dp", "tensor"),
            P(),
            P(),
        ),
        out_specs=P("dp", "tensor"),
        check_vma=False,
    )
```

```python
import functools

import jax
import jax.numpy as jnp
from jax import lax
from jax.experimental import pallas as pl
from jax.experimental.pallas import tpu as pltpu
from jax.sharding import PartitionSpec as P

DH = 128
TPD = 256
BLOCK = 64


EPS = 1e-06


def layer_norm(rows, gain):
    values = rows.astype(jnp.float32)
    mean = jnp.mean(values, axis=-1, keepdims=True)
    mean_sq = jnp.mean(values * values, axis=-1, keepdims=True)
    return (values - mean) * lax.rsqrt(mean_sq - mean * mean + EPS) * gain


def head_norm(values, gain):
    mean_sq = jnp.mean(values * values, axis=-1, keepdims=True)
    return values * lax.rsqrt(mean_sq + EPS) * gain


def add_rows(normed, piece):
    return jnp.dot(normed, piece, preferred_element_type=jnp.float32)


def allowed_pairs(block_mask):
    blocks = block_mask.shape[-1]
    allowed = (block_mask > 0) | (jnp.arange(blocks)[:, None] == jnp.arange(blocks)[None, :])[None]
    return jnp.repeat(jnp.repeat(allowed, BLOCK, axis=1), BLOCK, axis=2)


def per_device(tokens, block_mask, norm_gain, w_query, w_key, w_value, query_gain, key_gain):
    whole = lax.all_gather(tokens, "tensor", axis=1, tiled=True)
    normed = layer_norm(whole, norm_gain).astype(jnp.bfloat16)

    def add_one(piece):
        return add_rows(normed, piece)

    query = add_one(lax.all_gather(w_query, "dp", axis=0, tiled=True))
    key = add_one(lax.all_gather(w_key, "dp", axis=0, tiled=True))
    value = add_one(lax.all_gather(w_value, "dp", axis=0, tiled=True))
    draws_here = tokens.shape[0] // TPD
    heads_here = w_query.shape[1] // DH
    query_n = head_norm(query.reshape(draws_here, TPD, heads_here, DH), query_gain).astype(
        jnp.bfloat16
    )
    key_n = head_norm(key.reshape(draws_here, TPD, heads_here, DH), key_gain).astype(jnp.bfloat16)
    value = value.astype(jnp.bfloat16).reshape(draws_here, TPD, heads_here, DH)
    allowed = allowed_pairs(block_mask)
    scores = jnp.einsum(
        "bqhe,bkhe->bhqk", query_n, key_n, preferred_element_type=jnp.float32
    ) / jnp.sqrt(jnp.float32(DH))
    scores = jnp.where(allowed[:, None], scores, jnp.float32(-1e30))
    top = jnp.max(scores, axis=-1, keepdims=True)
    weights = jnp.exp(scores - top)
    probs = (weights / jnp.sum(weights, axis=-1, keepdims=True)).astype(jnp.bfloat16)
    out = jnp.einsum("bhqk,bkhe->bqhe", probs, value, preferred_element_type=jnp.float32)
    return out.astype(jnp.bfloat16).reshape(tokens.shape[0], heads_here * DH)


CORE, X, Y = 1, 2, 4

PLACES = ((0, 1, 2, 3), (1, 0, 2, 3), (2, 3, 1, 0), (3, 2, 1, 0))
OWN, PARTNER, MIDDLE, OUTWARD, MIDDLE_AGAIN, OUTWARD_AGAIN = range(6)
AT_ENDS = (OWN, PARTNER, OUTWARD, OUTWARD_AGAIN)
IN_MIDDLE = (OWN, PARTNER, MIDDLE, MIDDLE_AGAIN)
ARRIVALS = (AT_ENDS, IN_MIDDLE, IN_MIDDLE, AT_ENDS)
TO_PARTNER = ((0, 1), (1, 0), (2, 3), (3, 2))
TO_MIDDLE = ((1, 2), (2, 1))
TO_OUTSIDE = ((1, 0), (2, 3))


def plan(z, chip):
    diagonal = chip ^ 3
    order = [place for place in PLACES[z] if place != diagonal] + [diagonal]
    pairs = [number for place in order for number in (PLACES[z].index(place), place ^ chip)]
    return pairs + list(PLACES[z]) + list(ARRIVALS[z])


PLAN = [[plan(z, chip) for chip in range(4)] for z in range(4)]
PLACE, ARRIVAL, CORE_AT = 8, 12, 16

HBM = pl.BlockSpec(memory_space=pltpu.HBM)
ANY = pl.BlockSpec(memory_space=pl.ANY)
VMEM = pl.BlockSpec(memory_space=pltpu.VMEM)
SMEM = pl.BlockSpec(memory_space=pltpu.SMEM)
FREE = pl.CostEstimate(flops=0, bytes_accessed=0, transcendentals=0)


def params(mib):
    return pltpu.CompilerParams(vmem_limit_bytes=mib * 2**20)


def swap(array, bits):
    return lax.ppermute(array, "dp", [(i, i ^ bits) for i in range(8)])


def trade(array):
    return lax.all_to_all(array, "dp", 0, 0, axis_index_groups=[[i, i + 1] for i in range(0, 8, 2)])


def gate(arrays, others):
    return pl.pallas_call(
        lambda *refs: None,
        in_specs=[ANY] * (len(arrays) + len(others)),
        out_specs=[ANY] * len(arrays),
        out_shape=[jax.ShapeDtypeStruct(array.shape, array.dtype) for array in arrays],
        input_output_aliases={number: number for number in range(len(arrays))},
        compiler_params=params(1),
        cost_estimate=FREE,
    )(*arrays, *others)


def columns_of(heads):
    query = [h * 2 * DH for h in range(heads)]
    value = [heads * 2 * DH + h * DH for h in range(heads)]
    return query, [first + DH for first in query], value


def column_groups(width):
    return [(first, min(first + 2 * DH, width)) for first in range(0, width, 2 * DH)]


def pack_kernel(theirs, *refs):
    weights, out_ref, held, in_sems = refs[:3], *refs[-3:]
    core = lax.axis_index("dp") % 2
    width = held.shape[2]
    heads = width // DH

    def load(kind):
        first = pl.multiple_of((1 - core if theirs else core) * width, DH)
        return pltpu.make_async_copy(
            weights[kind].at[:, pl.ds(first, width)], held.at[kind], in_sems.at[kind]
        )

    for kind in range(3):
        load(kind).start()
    for kind, firsts in enumerate(columns_of(heads)):
        load(kind).wait()
        for h, first in enumerate(firsts):
            out_ref[:, first : first + DH] = held[kind, :, h * DH : (h + 1) * DH]


def pack(theirs, weights, *others):
    rows, columns = weights[0].shape
    return pl.pallas_call(
        functools.partial(pack_kernel, theirs),
        in_specs=[HBM] * 3 + [ANY] * len(others),
        out_specs=VMEM,
        out_shape=jax.ShapeDtypeStruct((rows, 3 * columns // 2), jnp.bfloat16),
        scratch_shapes=[
            pltpu.VMEM((3, rows, columns // 2), jnp.bfloat16),
            pltpu.SemaphoreType.DMA((3,)),
        ],
        compiler_params=params(56),
        cost_estimate=FREE,
    )(*weights, *others)


def fetch(chosen, choices, target, sem):
    for number, choice in choices.items():

        @pl.when(chosen == number)
        def _():
            pltpu.make_async_copy(choice, target, sem).start()


def norm_kernel(slots, numbers, plan_ref, stats_ref, gains_ref, *refs):
    arrays = dict(zip(numbers, refs))
    out_ref, raw, scratch, columns, in_sems, out_sems = refs[-6:]
    _, rows, features = raw.shape
    step = 64
    copies = out_ref.shape[0]
    normed = out_ref.at[0] if copies == 1 else scratch
    for n, slot in enumerate(slots):
        fetch(plan_ref[ARRIVAL + slot], arrays, raw.at[n], in_sems.at[n])
    stats = jnp.sum(stats_ref[...], axis=0) / (4 * features)
    mean = stats[0:1]
    scale = lax.rsqrt(stats[1:2] - mean * mean + EPS)
    columns[...] = jnp.concatenate([mean, scale, jnp.zeros((6, rows), jnp.float32)], axis=0).T
    for n, slot in enumerate(slots):
        gain = gains_ref[:, pl.ds(pl.multiple_of(plan_ref[PLACE + slot] * features, features), features)]
        pltpu.make_async_copy(refs[0], raw.at[n], in_sems.at[n]).wait()

        @pl.loop(0, rows // step)
        def _(tile):
            at = pl.ds(pl.multiple_of(tile * step, step), step)
            values = raw[n, at, :].astype(jnp.float32)
            normed[n, at, :] = ((values - columns[at, 0:1]) * columns[at, 1:2] * gain).astype(jnp.bfloat16)

        for copy in range(copies if copies > 1 else 0):
            pltpu.make_async_copy(normed.at[n], out_ref.at[copy, n], out_sems.at[copy, n]).start()
    for n in range(len(slots)):
        for copy in range(copies if copies > 1 else 0):
            pltpu.make_async_copy(normed.at[n], out_ref.at[copy, n], out_sems.at[copy, n]).wait()


def norm(plan_here, slots, copies, stats, gains, arrays, *others):
    rows, features = next(iter(arrays.values())).shape
    shape = (len(slots), rows, features)
    return pl.pallas_call(
        functools.partial(norm_kernel, slots, tuple(arrays)),
        in_specs=[SMEM] + [VMEM] * 2 + [ANY] * (len(arrays) + len(others)),
        out_specs=VMEM if copies == 1 else HBM,
        out_shape=jax.ShapeDtypeStruct((copies, *shape), jnp.bfloat16),
        scratch_shapes=[
            pltpu.VMEM(shape, jnp.bfloat16),
            pltpu.VMEM(shape if copies > 1 else (1, 16, 128), jnp.bfloat16),
            pltpu.VMEM((rows, 8), jnp.float32),
            pltpu.SemaphoreType.DMA((len(slots),)),
            pltpu.SemaphoreType.DMA((copies, len(slots))),
        ],
        compiler_params=params(16),
        cost_estimate=FREE,
    )(plan_here, stats, gains, *arrays.values(), *others)


class Tokens:
    def __init__(self, arrays):
        self.arrays = arrays
        _, _, self.rows, self.features = self.arrays[0].shape
        self.tiles_here = self.rows // TPD
        self.count = 2 * self.tiles_here

    def tiles(self, core, refs):
        found = [{} for _ in range(self.count)]
        slot = 0
        for ref, array in zip(refs, self.arrays):
            for n in range(array.shape[1]):
                for tile, choices in enumerate(found):
                    whose = core if tile < self.tiles_here else 1 - core
                    choices[slot] = ref.at[whose, n, pl.ds(tile % self.tiles_here * TPD, TPD)]
                slot += 1
        return found, refs[len(self.arrays) :]


def weight_copies(core, pair, columns, target, sems):
    copies = []
    for part, source in enumerate(pair):
        depth = source.shape[0]
        first = pl.multiple_of((core if part == 0 else 1 - core) * depth, depth)
        at = pl.ds(columns[0], columns[1] - columns[0])
        copies.append(
            pltpu.make_async_copy(source.at[:, at], target.at[pl.ds(first, depth), at], sems.at[part])
        )
    return copies


def weight_group(core, chosen, choices, columns, target, sems):
    def start():
        for number, pair in choices.items():

            @pl.when(chosen == number)
            def _():
                for copy in weight_copies(core, pair, columns, target, sems):
                    copy.start()

    def wait():
        for copy in weight_copies(core, choices[0], columns, target, sems):
            copy.wait()

    return [(start, wait)]


def token_group(chosen, views, target, sem):
    return [(functools.partial(fetch, chosen, views, target, sem), pltpu.make_async_copy(views[0], target, sem).wait)]


def run(groups, steps, ahead):
    started = waited = 0
    for need, step in steps:
        while started < min(need + 1 + ahead, len(groups)):
            for start, _ in groups[started]:
                start()
            started += 1
        while waited <= need:
            for _, wait in groups[waited]:
                wait()
            waited += 1
        step()


def project_kernel(tokens_of, plan_ref, *refs):
    core = plan_ref[CORE_AT]
    tiles, refs = tokens_of.tiles(core, refs)
    choices = {0: (refs[0].at[core], refs[0].at[1 - core]), 1: (refs[1], refs[2]), 2: (refs[3], refs[4])}
    total, next_tokens, next_weights, tokens, weights, token_sems, weight_sems, next_sems = refs[5:]
    count, _, width = weights.shape
    cuts = [0, 2 * DH, 4 * DH, 6 * DH, width]

    def add(n, first, last, tile):
        update = jnp.dot(tokens[n, tile], weights[n, :, first:last], preferred_element_type=jnp.float32)
        if n > 0:
            update = update + total[tile, :, first:last]
        total[tile, :, first:last] = update

    groups, steps = [], []
    for n in range(count):
        slot, bits = plan_ref[2 * n], plan_ref[2 * n + 1]
        for piece, columns in enumerate(zip(cuts, cuts[1:])):
            group = weight_group(core, bits, choices, columns, weights.at[n], weight_sems.at[n, piece])
            if piece > 0:
                groups.append(group)
            for tile, views in enumerate(tiles):
                if piece == 0:
                    tile_group = token_group(slot, views, tokens.at[n, tile], token_sems.at[n, tile])
                    groups.append(group + tile_group if tile == 0 else tile_group)
                for first, last in column_groups(width):
                    if columns[0] <= first < columns[1]:
                        steps.append((len(groups) - 1, functools.partial(add, n, first, last, tile)))
    slot = jnp.where(plan_ref[4] == 3, plan_ref[6], plan_ref[4])
    for tile, views in enumerate(tiles):
        groups.append(token_group(slot, views, next_tokens.at[tile], token_sems.at[count, tile]))
    groups.append(weight_group(core, plan_ref[5], choices, (0, width), next_weights, next_sems))
    steps.append((len(groups) - 1, lambda: None))
    run(groups, steps, 5)


def project(plan_here, arrays, near):
    tokens = Tokens(arrays)
    depth, width = near[1].shape
    count = 2
    shape = (tokens.count, TPD, tokens.features)
    return pl.pallas_call(
        functools.partial(project_kernel, tokens),
        in_specs=[SMEM] + [HBM] * (len(arrays) + len(near)),
        out_specs=[VMEM] * 3,
        out_shape=[
            jax.ShapeDtypeStruct((tokens.count, TPD, width), jnp.float32),
            jax.ShapeDtypeStruct(shape, jnp.bfloat16),
            jax.ShapeDtypeStruct((tokens.features, width), jnp.bfloat16),
        ],
        scratch_shapes=[
            pltpu.VMEM((count, *shape), jnp.bfloat16),
            pltpu.VMEM((count, tokens.features, width), jnp.bfloat16),
            pltpu.SemaphoreType.DMA((count + 1, tokens.count)),
            pltpu.SemaphoreType.DMA((count, 4, 2)),
            pltpu.SemaphoreType.DMA((2,)),
        ],
        compiler_params=params(18),
        cost_estimate=FREE,
    )(plan_here, *arrays, *near)


def attend(query, key, value, mask_ref, draw):
    scores = lax.dot_general(
        query, key, (((1,), (1,)), ((), ())), preferred_element_type=jnp.float32
    )
    weights = jnp.exp(scores * (DH**-0.5))
    blocks = TPD // BLOCK
    column = lax.broadcasted_iota(jnp.int32, (1, TPD), 1) // BLOCK
    bands = []
    for i in range(blocks):
        allowed = column == i
        for j in range(blocks):
            allowed = allowed | ((column == j) & (mask_ref[(draw * blocks + i) * blocks + j] > 0))
        bands.append(jnp.where(allowed, weights[i * BLOCK : (i + 1) * BLOCK], 0.0))
    weights = jnp.concatenate(bands, axis=0).astype(jnp.bfloat16)
    both = jnp.dot(
        weights,
        jnp.concatenate([value, jnp.ones_like(value)], axis=1),
        preferred_element_type=jnp.float32,
    )
    return (both[:, :DH] / both[:, DH:]).astype(jnp.bfloat16)


def place(plan_ref, side, next_tokens, last_ref, near_tokens=None, diag_tokens=None):
    core = plan_ref[CORE_AT]
    tiles = last_ref.shape[2] // TPD

    def copy(near, diag):
        if near_tokens is not None:
            near_tokens[...] = near(slice(None))
        if diag_tokens is not None:
            depth = diag_tokens.shape[2]
            for part in range(2):
                first = pl.multiple_of((core if part == 0 else 1 - core) * depth, depth)
                diag_tokens[part] = diag(pl.ds(first, depth))

    def last(features):
        return last_ref[0, 0, :, features]

    def early(features):
        chunk = next_tokens[side * tiles : (side + 1) * tiles, :, features]
        return chunk.reshape(tiles * TPD, chunk.shape[2])

    @pl.when(plan_ref[4] == 3)
    def _():
        copy(last, early)

    @pl.when(plan_ref[4] != 3)
    def _():
        copy(early, last)


def near_kernel(side, plan_ref, total_ref, next_tokens, next_weights, last_ref, *refs):
    out_ref, near_tokens = refs[-2:]
    place(plan_ref, side, next_tokens, last_ref, near_tokens=near_tokens)
    tiles, _, width = out_ref.shape
    for tile in range(tiles):
        rows = near_tokens[tile * TPD : (tile + 1) * TPD, :]
        for first, end in column_groups(width):
            out_ref[tile, :, first:end] = total_ref[side * tiles + tile, :, first:end] + jnp.dot(
                rows, next_weights[:, first:end], preferred_element_type=jnp.float32
            )


def add_near(side, plan_here, total, next_tokens, next_weights, last):
    tiles, _, width = total.shape
    _, _, rows, features = last.shape
    return pl.pallas_call(
        functools.partial(near_kernel, side),
        in_specs=[SMEM] + [VMEM] * 4,
        out_specs=VMEM,
        out_shape=jax.ShapeDtypeStruct((tiles // 2, TPD, width), jnp.float32),
        scratch_shapes=[pltpu.VMEM((rows, features), jnp.bfloat16)],
        compiler_params=params(18),
        cost_estimate=FREE,
    )(plan_here, total, next_tokens, next_weights, last)


def finish_kernel(
    side,
    first_tile,
    plan_ref,
    mask_ref,
    total_ref,
    next_tokens,
    last_ref,
    diag_same,
    diag_cross,
    query_gain,
    key_gain,
    *refs,
):
    out_ref, near_tokens, diag_tokens = refs[-3:]
    core = plan_ref[CORE_AT]
    width = total_ref.shape[2]
    heads = width // (3 * DH)
    tiles = last_ref.shape[2] // TPD
    near = near_tokens.shape[0] > TPD
    place(plan_ref, side, next_tokens, last_ref, near_tokens if near else None, diag_tokens)
    query_first, key_first, value_first = columns_of(heads)
    for tile in range(tiles):
        sums = []
        at = slice(tile * TPD, (tile + 1) * TPD)
        pairs = [(diag_tokens[0, at], diag_same), (diag_tokens[1, at], diag_cross)]
        if near:
            pairs.append((near_tokens[at, :], refs[0]))
        for first, end in column_groups(width):
            part = total_ref[first_tile + tile, :, first:end]
            for tokens, weights in pairs:
                part = part + jnp.dot(tokens, weights[:, first:end], preferred_element_type=jnp.float32)
            sums += [part[:, column : column + DH] for column in range(0, end - first, DH)]
        whose = core if side == 0 else 1 - core
        for h in range(heads):
            query = head_norm(sums[query_first[h] // DH], query_gain[...]).astype(jnp.bfloat16)
            key = head_norm(sums[key_first[h] // DH], key_gain[...]).astype(jnp.bfloat16)
            value = sums[value_first[h] // DH].astype(jnp.bfloat16)
            out_ref[at, h * DH : (h + 1) * DH] = attend(query, key, value, mask_ref, whose * tiles + tile)


def finish(side, plan_here, mask, total, next_tokens, last, diag, gains, next_weights=None, others=()):
    width = total.shape[2]
    _, _, rows, features = last.shape
    near = next_weights is not None
    return pl.pallas_call(
        functools.partial(finish_kernel, side, side * rows // TPD if near else 0),
        in_specs=[SMEM] * 2 + [VMEM] * (8 if near else 7) + [ANY] * len(others),
        out_specs=VMEM,
        out_shape=jax.ShapeDtypeStruct((rows, width // 3), jnp.bfloat16),
        scratch_shapes=[
            pltpu.VMEM((rows if near else 16, features), jnp.bfloat16),
            pltpu.VMEM((2, rows, diag[0].shape[0]), jnp.bfloat16),
        ],
        compiler_params=params(18),
        cost_estimate=FREE,
    )(plan_here, mask, total, next_tokens, last, *diag, *gains, *([next_weights] if near else []), *others)


def per_device_8x4(tokens, block_mask, norm_gain, w_query, w_key, w_value, query_gain, key_gain):
    features = tokens.shape[1]
    heads = w_query.shape[1] // (2 * DH)
    dp, z = lax.axis_index("dp"), lax.axis_index("tensor")
    core = (dp % 2).astype(jnp.int32)
    plan_here = jnp.asarray(PLAN, jnp.int32)[z, dp // 2]
    plan_here = jnp.concatenate([plan_here, core[None]])

    def along(array, pairs):
        return lax.ppermute(array, "tensor", pairs)

    mine = pack(False, (w_query, w_key, w_value))
    x_same, y_same = swap(mine, X), swap(mine, Y)
    partner, middle = along(tokens, TO_PARTNER), along(tokens, TO_MIDDLE)
    values = tokens.astype(jnp.float32)
    stats = jnp.stack([jnp.sum(values, axis=1), jnp.sum(values * values, axis=1)])
    other = pack(True, (w_query, w_key, w_value), mine)
    own = trade(jnp.where(core == 0, jnp.stack([mine, other]), jnp.stack([other, mine])))
    mask = block_mask.astype(jnp.float32).reshape(1, -1)
    mask = trade(jnp.concatenate([mask, mask])).reshape(-1)
    (stats,) = gate((stats,), (own, mask))
    stats = lax.all_to_all(jnp.stack([stats] * 4), "tensor", 0, 0)
    gains = norm_gain.reshape(1, -1)

    other, partner, middle, stats = gate((other, partner, middle, stats), (x_same, y_same))
    x_cross, y_cross = swap(other, X | CORE), swap(other, Y | CORE)
    outward, middle_again = along(middle, TO_OUTSIDE), along(partner, TO_MIDDLE)

    arrived = {OWN: tokens, PARTNER: partner}
    normed = [trade(norm(plan_here, (0, 1), 2, stats, gains, arrived))]

    x_same, y_cross, outward, middle_again = gate(
        (x_same, y_cross, outward, middle_again), (x_cross, normed[0])
    )
    diag_same, diag_cross = swap(x_same, Y), swap(y_cross, X)
    outward_again = along(middle_again, TO_OUTSIDE)
    arrived = {MIDDLE: middle, OUTWARD: outward}
    normed.append(trade(norm(plan_here, (2,), 2, stats, gains, arrived)))
    near = [own, x_same, x_cross, y_same, y_cross]
    total, next_tokens, next_weights = project(plan_here, normed, near)

    arrived = {MIDDLE_AGAIN: middle_again, OUTWARD_AGAIN: outward_again}
    last = norm(plan_here, (3,), 1, stats, gains, arrived, total)
    diag = (diag_same, diag_cross)
    gain_pair = (query_gain[None, :], key_gain[None, :])
    last_there = swap(last, CORE)
    total_here = add_near(0, plan_here, total, next_tokens, next_weights, last)
    (last_there,) = gate((last_there,), (total_here,))
    theirs = finish(1, plan_here, mask, total, next_tokens, last_there, diag, gain_pair, next_weights)
    here = finish(0, plan_here, mask, total_here, next_tokens, last, diag, gain_pair, others=(theirs,))
    there = swap(theirs, CORE)
    return jnp.where(
        core == 0,
        jnp.concatenate([here, there], axis=1),
        jnp.concatenate([there, here], axis=1),
    )


def solution(mesh):
    eight_by_four = dict(mesh.shape) == {"dp": 8, "tensor": 4}
    return jax.shard_map(
        per_device_8x4 if eight_by_four else per_device,
        mesh=mesh,
        in_specs=(
            P("dp", "tensor"),
            P("dp", None, None),
            P(),
            P("dp", "tensor"),
            P("dp", "tensor"),
            P("dp", "tensor"),
            P(),
            P(),
        ),
        out_specs=P("dp", "tensor"),
        check_vma=False,
    )
```

```python
import functools

import jax
import jax.numpy as jnp
from jax import lax
from jax.experimental import pallas as pl
from jax.experimental.pallas import tpu as pltpu
from jax.sharding import PartitionSpec as P

DH = 128
TPD = 256
BLOCK = 64


EPS = 1e-06


def layer_norm(rows, gain):
    values = rows.astype(jnp.float32)
    mean = jnp.mean(values, axis=-1, keepdims=True)
    mean_sq = jnp.mean(values * values, axis=-1, keepdims=True)
    return (values - mean) * lax.rsqrt(mean_sq - mean * mean + EPS) * gain


def head_norm(values, gain):
    mean_sq = jnp.mean(values * values, axis=-1, keepdims=True)
    return values * lax.rsqrt(mean_sq + EPS) * gain


def add_rows(normed, piece):
    return jnp.dot(normed, piece, preferred_element_type=jnp.float32)


def allowed_pairs(block_mask):
    blocks = block_mask.shape[-1]
    allowed = (block_mask > 0) | (jnp.arange(blocks)[:, None] == jnp.arange(blocks)[None, :])[None]
    return jnp.repeat(jnp.repeat(allowed, BLOCK, axis=1), BLOCK, axis=2)


def per_device(tokens, block_mask, norm_gain, w_query, w_key, w_value, query_gain, key_gain):
    whole = lax.all_gather(tokens, "tensor", axis=1, tiled=True)
    normed = layer_norm(whole, norm_gain).astype(jnp.bfloat16)

    def add_one(piece):
        return add_rows(normed, piece)

    query = add_one(lax.all_gather(w_query, "dp", axis=0, tiled=True))
    key = add_one(lax.all_gather(w_key, "dp", axis=0, tiled=True))
    value = add_one(lax.all_gather(w_value, "dp", axis=0, tiled=True))
    draws_here = tokens.shape[0] // TPD
    heads_here = w_query.shape[1] // DH
    query_n = head_norm(query.reshape(draws_here, TPD, heads_here, DH), query_gain).astype(
        jnp.bfloat16
    )
    key_n = head_norm(key.reshape(draws_here, TPD, heads_here, DH), key_gain).astype(jnp.bfloat16)
    value = value.astype(jnp.bfloat16).reshape(draws_here, TPD, heads_here, DH)
    allowed = allowed_pairs(block_mask)
    scores = jnp.einsum(
        "bqhe,bkhe->bhqk", query_n, key_n, preferred_element_type=jnp.float32
    ) / jnp.sqrt(jnp.float32(DH))
    scores = jnp.where(allowed[:, None], scores, jnp.float32(-1e30))
    top = jnp.max(scores, axis=-1, keepdims=True)
    weights = jnp.exp(scores - top)
    probs = (weights / jnp.sum(weights, axis=-1, keepdims=True)).astype(jnp.bfloat16)
    out = jnp.einsum("bhqk,bkhe->bqhe", probs, value, preferred_element_type=jnp.float32)
    return out.astype(jnp.bfloat16).reshape(tokens.shape[0], heads_here * DH)


CORE, X, Y = 1, 2, 4

PLACES = ((0, 1, 2, 3), (1, 0, 2, 3), (2, 3, 1, 0), (3, 2, 1, 0))
OWN, PARTNER, MIDDLE, OUTWARD, MIDDLE_AGAIN, OUTWARD_AGAIN = range(6)
AT_ENDS = (OWN, PARTNER, OUTWARD, OUTWARD_AGAIN)
IN_MIDDLE = (OWN, PARTNER, MIDDLE, MIDDLE_AGAIN)
ARRIVALS = (AT_ENDS, IN_MIDDLE, IN_MIDDLE, AT_ENDS)
TO_PARTNER = ((0, 1), (1, 0), (2, 3), (3, 2))
TO_MIDDLE = ((1, 2), (2, 1))
TO_OUTSIDE = ((1, 0), (2, 3))


def plan(z, chip):
    diagonal = chip ^ 3
    order = [place for place in PLACES[z] if place != diagonal] + [diagonal]
    pairs = [number for place in order for number in (PLACES[z].index(place), place ^ chip)]
    return pairs + list(PLACES[z]) + list(ARRIVALS[z])


PLAN = [[plan(z, chip) for chip in range(4)] for z in range(4)]
PLACE, ARRIVAL, CORE_AT = 8, 12, 16

HBM = pl.BlockSpec(memory_space=pltpu.HBM)
ANY = pl.BlockSpec(memory_space=pl.ANY)
VMEM = pl.BlockSpec(memory_space=pltpu.VMEM)
SMEM = pl.BlockSpec(memory_space=pltpu.SMEM)
FREE = pl.CostEstimate(flops=0, bytes_accessed=0, transcendentals=0)


def params(mib):
    return pltpu.CompilerParams(vmem_limit_bytes=mib * 2**20)


def swap(array, bits):
    return lax.ppermute(array, "dp", [(i, i ^ bits) for i in range(8)])


def trade(array):
    return lax.all_to_all(array, "dp", 0, 0, axis_index_groups=[[i, i + 1] for i in range(0, 8, 2)])


def gate(arrays, others):
    return pl.pallas_call(
        lambda *refs: None,
        in_specs=[ANY] * (len(arrays) + len(others)),
        out_specs=[ANY] * len(arrays),
        out_shape=[jax.ShapeDtypeStruct(array.shape, array.dtype) for array in arrays],
        input_output_aliases={number: number for number in range(len(arrays))},
        compiler_params=params(1),
        cost_estimate=FREE,
    )(*arrays, *others)


def columns_of(heads):
    query = [h * 2 * DH for h in range(heads)]
    value = [heads * 2 * DH + h * DH for h in range(heads)]
    return query, [first + DH for first in query], value


def column_groups(width):
    return [(first, min(first + 2 * DH, width)) for first in range(0, width, 2 * DH)]


def pack_kernel(theirs, *refs):
    weights, out_ref, held, packed, in_sems, out_sems = refs[:3], *refs[-5:]
    core = lax.axis_index("dp") % 2
    width = held.shape[2]
    heads = width // DH

    def load(kind):
        first = pl.multiple_of((1 - core if theirs else core) * width, DH)
        return pltpu.make_async_copy(
            weights[kind].at[:, pl.ds(first, width)], held.at[kind], in_sems.at[kind]
        )

    def store(number):
        at = pl.ds(0, 2 * width) if number == 0 else pl.ds(2 * width, width)
        return pltpu.make_async_copy(packed.at[:, at], out_ref.at[:, at], out_sems.at[number])

    for kind in range(3):
        load(kind).start()
    for kind, firsts in enumerate(columns_of(heads)):
        load(kind).wait()
        for h, first in enumerate(firsts):
            packed[:, first : first + DH] = held[kind, :, h * DH : (h + 1) * DH]
        if kind > 0:
            store(kind - 1).start()
    for number in range(2):
        store(number).wait()


def pack(theirs, weights, *others):
    rows, columns = weights[0].shape
    shape = (rows, 3 * columns // 2)
    return pl.pallas_call(
        functools.partial(pack_kernel, theirs),
        in_specs=[HBM] * 3 + [ANY] * len(others),
        out_specs=HBM,
        out_shape=jax.ShapeDtypeStruct(shape, jnp.bfloat16),
        scratch_shapes=[
            pltpu.VMEM((3, rows, columns // 2), jnp.bfloat16),
            pltpu.VMEM(shape, jnp.bfloat16),
            pltpu.SemaphoreType.DMA((3,)),
            pltpu.SemaphoreType.DMA((2,)),
        ],
        compiler_params=params(56),
        cost_estimate=FREE,
    )(*weights, *others)


def fetch(chosen, choices, target, sem):
    for number, choice in choices.items():

        @pl.when(chosen == number)
        def _():
            pltpu.make_async_copy(choice, target, sem).start()


def norm_kernel(slots, numbers, plan_ref, stats_ref, gains_ref, *refs):
    arrays = dict(zip(numbers, refs))
    out_ref, raw, scratch, columns, in_sems, out_sems = refs[-6:]
    _, rows, features = raw.shape
    step = 64
    copies = out_ref.shape[0]
    normed = out_ref.at[0] if copies == 1 else scratch
    for n, slot in enumerate(slots):
        fetch(plan_ref[ARRIVAL + slot], arrays, raw.at[n], in_sems.at[n])
    stats = jnp.sum(stats_ref[...], axis=0) / (4 * features)
    mean = stats[0:1]
    scale = lax.rsqrt(stats[1:2] - mean * mean + EPS)
    columns[...] = jnp.concatenate([mean, scale, jnp.zeros((6, rows), jnp.float32)], axis=0).T
    for n, slot in enumerate(slots):
        gain = gains_ref[:, pl.ds(pl.multiple_of(plan_ref[PLACE + slot] * features, features), features)]
        pltpu.make_async_copy(refs[0], raw.at[n], in_sems.at[n]).wait()

        @pl.loop(0, rows // step)
        def _(tile):
            at = pl.ds(pl.multiple_of(tile * step, step), step)
            values = raw[n, at, :].astype(jnp.float32)
            normed[n, at, :] = ((values - columns[at, 0:1]) * columns[at, 1:2] * gain).astype(jnp.bfloat16)

        for copy in range(copies if copies > 1 else 0):
            pltpu.make_async_copy(normed.at[n], out_ref.at[copy, n], out_sems.at[copy, n]).start()
    for n in range(len(slots)):
        for copy in range(copies if copies > 1 else 0):
            pltpu.make_async_copy(normed.at[n], out_ref.at[copy, n], out_sems.at[copy, n]).wait()


def norm(plan_here, slots, copies, stats, gains, arrays, *others):
    rows, features = next(iter(arrays.values())).shape
    shape = (len(slots), rows, features)
    return pl.pallas_call(
        functools.partial(norm_kernel, slots, tuple(arrays)),
        in_specs=[SMEM] + [VMEM] * 2 + [ANY] * (len(arrays) + len(others)),
        out_specs=VMEM if copies == 1 else HBM,
        out_shape=jax.ShapeDtypeStruct((copies, *shape), jnp.bfloat16),
        scratch_shapes=[
            pltpu.VMEM(shape, jnp.bfloat16),
            pltpu.VMEM(shape if copies > 1 else (1, 16, 128), jnp.bfloat16),
            pltpu.VMEM((rows, 8), jnp.float32),
            pltpu.SemaphoreType.DMA((len(slots),)),
            pltpu.SemaphoreType.DMA((copies, len(slots))),
        ],
        compiler_params=params(16),
        cost_estimate=FREE,
    )(plan_here, stats, gains, *arrays.values(), *others)


class Tokens:
    def __init__(self, arrays):
        self.arrays = arrays
        _, _, self.rows, self.features = self.arrays[0].shape
        self.tiles_here = self.rows // TPD
        self.count = 2 * self.tiles_here

    def tiles(self, core, refs):
        found = [{} for _ in range(self.count)]
        slot = 0
        for ref, array in zip(refs, self.arrays):
            for n in range(array.shape[1]):
                for tile, choices in enumerate(found):
                    whose = core if tile < self.tiles_here else 1 - core
                    choices[slot] = ref.at[whose, n, pl.ds(tile % self.tiles_here * TPD, TPD)]
                slot += 1
        return found, refs[len(self.arrays) :]


def weight_copies(core, pair, columns, target, sems):
    copies = []
    for part, source in enumerate(pair):
        depth = source.shape[0]
        first = pl.multiple_of((core if part == 0 else 1 - core) * depth, depth)
        at = pl.ds(columns[0], columns[1] - columns[0])
        copies.append(
            pltpu.make_async_copy(source.at[:, at], target.at[pl.ds(first, depth), at], sems.at[part])
        )
    return copies


def weight_group(core, chosen, choices, columns, target, sems):
    def start():
        for number, pair in choices.items():

            @pl.when(chosen == number)
            def _():
                for copy in weight_copies(core, pair, columns, target, sems):
                    copy.start()

    def wait():
        for copy in weight_copies(core, choices[0], columns, target, sems):
            copy.wait()

    return [(start, wait)]


def token_group(chosen, views, target, sem):
    return [(functools.partial(fetch, chosen, views, target, sem), pltpu.make_async_copy(views[0], target, sem).wait)]


def run(groups, steps, ahead):
    started = waited = 0
    for need, step in steps:
        while started < min(need + 1 + ahead, len(groups)):
            for start, _ in groups[started]:
                start()
            started += 1
        while waited <= need:
            for _, wait in groups[waited]:
                wait()
            waited += 1
        step()


def project_kernel(tokens_of, plan_ref, *refs):
    core = plan_ref[CORE_AT]
    tiles, refs = tokens_of.tiles(core, refs)
    choices = {0: (refs[0].at[core], refs[0].at[1 - core]), 1: (refs[1], refs[2]), 2: (refs[3], refs[4])}
    total, next_tokens, next_weights, tokens, weights, token_sems, weight_sems, next_sems = refs[5:]
    count, _, width = weights.shape
    cuts = [0, 2 * DH, 4 * DH, 6 * DH, width]

    def add(n, first, last, tile):
        update = jnp.dot(tokens[n, tile], weights[n, :, first:last], preferred_element_type=jnp.float32)
        if n > 0:
            update = update + total[tile, :, first:last]
        total[tile, :, first:last] = update

    groups, steps = [], []
    for n in range(count):
        slot, bits = plan_ref[2 * n], plan_ref[2 * n + 1]
        for piece, columns in enumerate(zip(cuts, cuts[1:])):
            group = weight_group(core, bits, choices, columns, weights.at[n], weight_sems.at[n, piece])
            if piece > 0:
                groups.append(group)
            for tile, views in enumerate(tiles):
                if piece == 0:
                    tile_group = token_group(slot, views, tokens.at[n, tile], token_sems.at[n, tile])
                    groups.append(group + tile_group if tile == 0 else tile_group)
                for first, last in column_groups(width):
                    if columns[0] <= first < columns[1]:
                        steps.append((len(groups) - 1, functools.partial(add, n, first, last, tile)))
    slot = jnp.where(plan_ref[4] == 3, plan_ref[6], plan_ref[4])
    for tile, views in enumerate(tiles):
        groups.append(token_group(slot, views, next_tokens.at[tile], token_sems.at[count, tile]))
    groups.append(weight_group(core, plan_ref[5], choices, (0, width), next_weights, next_sems))
    steps.append((len(groups) - 1, lambda: None))
    run(groups, steps, 5)


def project(plan_here, arrays, near):
    tokens = Tokens(arrays)
    depth, width = near[1].shape
    count = 2
    shape = (tokens.count, TPD, tokens.features)
    return pl.pallas_call(
        functools.partial(project_kernel, tokens),
        in_specs=[SMEM] + [HBM] * (len(arrays) + len(near)),
        out_specs=[VMEM] * 3,
        out_shape=[
            jax.ShapeDtypeStruct((tokens.count, TPD, width), jnp.float32),
            jax.ShapeDtypeStruct(shape, jnp.bfloat16),
            jax.ShapeDtypeStruct((tokens.features, width), jnp.bfloat16),
        ],
        scratch_shapes=[
            pltpu.VMEM((count, *shape), jnp.bfloat16),
            pltpu.VMEM((count, tokens.features, width), jnp.bfloat16),
            pltpu.SemaphoreType.DMA((count + 1, tokens.count)),
            pltpu.SemaphoreType.DMA((count, 4, 2)),
            pltpu.SemaphoreType.DMA((2,)),
        ],
        compiler_params=params(18),
        cost_estimate=FREE,
    )(plan_here, *arrays, *near)


def attend(query, key, value, mask_ref, draw):
    scores = lax.dot_general(
        query, key, (((1,), (1,)), ((), ())), preferred_element_type=jnp.float32
    )
    weights = jnp.exp(scores * (DH**-0.5))
    blocks = TPD // BLOCK
    column = lax.broadcasted_iota(jnp.int32, (1, TPD), 1) // BLOCK
    bands = []
    for i in range(blocks):
        allowed = column == i
        for j in range(blocks):
            allowed = allowed | ((column == j) & (mask_ref[(draw * blocks + i) * blocks + j] > 0))
        bands.append(jnp.where(allowed, weights[i * BLOCK : (i + 1) * BLOCK], 0.0))
    weights = jnp.concatenate(bands, axis=0).astype(jnp.bfloat16)
    both = jnp.dot(
        weights,
        jnp.concatenate([value, jnp.ones_like(value)], axis=1),
        preferred_element_type=jnp.float32,
    )
    return (both[:, :DH] / both[:, DH:]).astype(jnp.bfloat16)


def place(plan_ref, side, next_tokens, last_ref, near_tokens=None, diag_tokens=None):
    core = plan_ref[CORE_AT]
    tiles = last_ref.shape[2] // TPD

    def copy(near, diag):
        if near_tokens is not None:
            near_tokens[...] = near(slice(None))
        if diag_tokens is not None:
            depth = diag_tokens.shape[2]
            for part in range(2):
                first = pl.multiple_of((core if part == 0 else 1 - core) * depth, depth)
                diag_tokens[part] = diag(pl.ds(first, depth))

    def last(features):
        return last_ref[0, 0, :, features]

    def early(features):
        chunk = next_tokens[side * tiles : (side + 1) * tiles, :, features]
        return chunk.reshape(tiles * TPD, chunk.shape[2])

    @pl.when(plan_ref[4] == 3)
    def _():
        copy(last, early)

    @pl.when(plan_ref[4] != 3)
    def _():
        copy(early, last)


def near_kernel(side, plan_ref, total_ref, next_tokens, next_weights, last_ref, *refs):
    out_ref, near_tokens = refs[-2:]
    place(plan_ref, side, next_tokens, last_ref, near_tokens=near_tokens)
    tiles, _, width = out_ref.shape
    for tile in range(tiles):
        rows = near_tokens[tile * TPD : (tile + 1) * TPD, :]
        for first, end in column_groups(width):
            out_ref[tile, :, first:end] = total_ref[side * tiles + tile, :, first:end] + jnp.dot(
                rows, next_weights[:, first:end], preferred_element_type=jnp.float32
            )


def add_near(side, plan_here, total, next_tokens, next_weights, last):
    tiles, _, width = total.shape
    _, _, rows, features = last.shape
    return pl.pallas_call(
        functools.partial(near_kernel, side),
        in_specs=[SMEM] + [VMEM] * 4,
        out_specs=VMEM,
        out_shape=jax.ShapeDtypeStruct((tiles // 2, TPD, width), jnp.float32),
        scratch_shapes=[pltpu.VMEM((rows, features), jnp.bfloat16)],
        compiler_params=params(18),
        cost_estimate=FREE,
    )(plan_here, total, next_tokens, next_weights, last)


def finish_kernel(
    side,
    first_tile,
    plan_ref,
    mask_ref,
    total_ref,
    next_tokens,
    last_ref,
    diag_same,
    diag_cross,
    query_gain,
    key_gain,
    *refs,
):
    out_ref, near_tokens, diag_tokens = refs[-3:]
    core = plan_ref[CORE_AT]
    width = total_ref.shape[2]
    heads = width // (3 * DH)
    tiles = last_ref.shape[2] // TPD
    near = near_tokens.shape[0] > TPD
    place(plan_ref, side, next_tokens, last_ref, near_tokens if near else None, diag_tokens)
    query_first, key_first, value_first = columns_of(heads)
    for tile in range(tiles):
        sums = []
        at = slice(tile * TPD, (tile + 1) * TPD)
        pairs = [(diag_tokens[0, at], diag_same), (diag_tokens[1, at], diag_cross)]
        if near:
            pairs.append((near_tokens[at, :], refs[0]))
        for first, end in column_groups(width):
            part = total_ref[first_tile + tile, :, first:end]
            for tokens, weights in pairs:
                part = part + jnp.dot(tokens, weights[:, first:end], preferred_element_type=jnp.float32)
            sums += [part[:, column : column + DH] for column in range(0, end - first, DH)]
        whose = core if side == 0 else 1 - core
        for h in range(heads):
            query = head_norm(sums[query_first[h] // DH], query_gain[...]).astype(jnp.bfloat16)
            key = head_norm(sums[key_first[h] // DH], key_gain[...]).astype(jnp.bfloat16)
            value = sums[value_first[h] // DH].astype(jnp.bfloat16)
            out_ref[at, h * DH : (h + 1) * DH] = attend(query, key, value, mask_ref, whose * tiles + tile)


def finish(side, plan_here, mask, total, next_tokens, last, diag, gains, next_weights=None, others=()):
    width = total.shape[2]
    _, _, rows, features = last.shape
    near = next_weights is not None
    return pl.pallas_call(
        functools.partial(finish_kernel, side, side * rows // TPD if near else 0),
        in_specs=[SMEM] * 2 + [VMEM] * (8 if near else 7) + [ANY] * len(others),
        out_specs=VMEM,
        out_shape=jax.ShapeDtypeStruct((rows, width // 3), jnp.bfloat16),
        scratch_shapes=[
            pltpu.VMEM((rows if near else 16, features), jnp.bfloat16),
            pltpu.VMEM((2, rows, diag[0].shape[0]), jnp.bfloat16),
        ],
        compiler_params=params(18),
        cost_estimate=FREE,
    )(plan_here, mask, total, next_tokens, last, *diag, *gains, *([next_weights] if near else []), *others)


def per_device_8x4(tokens, block_mask, norm_gain, w_query, w_key, w_value, query_gain, key_gain):
    features = tokens.shape[1]
    heads = w_query.shape[1] // (2 * DH)
    dp, z = lax.axis_index("dp"), lax.axis_index("tensor")
    core = (dp % 2).astype(jnp.int32)
    plan_here = jnp.asarray(PLAN, jnp.int32)[z, dp // 2]
    plan_here = jnp.concatenate([plan_here, core[None]])

    def along(array, pairs):
        return lax.ppermute(array, "tensor", pairs)

    mine = pack(False, (w_query, w_key, w_value))
    x_same, y_same = swap(mine, X), swap(mine, Y)
    partner, middle = along(tokens, TO_PARTNER), along(tokens, TO_MIDDLE)
    values = tokens.astype(jnp.float32)
    stats = jnp.stack([jnp.sum(values, axis=1), jnp.sum(values * values, axis=1)])
    other = pack(True, (w_query, w_key, w_value), mine)
    own = trade(jnp.where(core == 0, jnp.stack([mine, other]), jnp.stack([other, mine])))
    mask = block_mask.astype(jnp.float32).reshape(1, -1)
    mask = trade(jnp.concatenate([mask, mask])).reshape(-1)
    (stats,) = gate((stats,), (own, mask))
    stats = lax.all_to_all(jnp.stack([stats] * 4), "tensor", 0, 0)
    gains = norm_gain.reshape(1, -1)

    other, partner, middle, stats = gate((other, partner, middle, stats), (x_same, y_same))
    x_cross, y_cross = swap(other, X | CORE), swap(other, Y | CORE)
    outward, middle_again = along(middle, TO_OUTSIDE), along(partner, TO_MIDDLE)

    arrived = {OWN: tokens, PARTNER: partner}
    normed = [trade(norm(plan_here, (0, 1), 2, stats, gains, arrived))]

    x_same, y_cross, outward, middle_again = gate(
        (x_same, y_cross, outward, middle_again), (x_cross, normed[0])
    )
    diag_same, diag_cross = swap(x_same, Y), swap(y_cross, X)
    outward_again = along(middle_again, TO_OUTSIDE)
    arrived = {MIDDLE: middle, OUTWARD: outward}
    normed.append(trade(norm(plan_here, (2,), 2, stats, gains, arrived)))
    near = [own, x_same, x_cross, y_same, y_cross]
    total, next_tokens, next_weights = project(plan_here, normed, near)

    arrived = {MIDDLE_AGAIN: middle_again, OUTWARD_AGAIN: outward_again}
    last = norm(plan_here, (3,), 1, stats, gains, arrived, total)
    diag = (diag_same, diag_cross)
    gain_pair = (query_gain[None, :], key_gain[None, :])
    last_there = swap(last, CORE)
    total_here = add_near(0, plan_here, total, next_tokens, next_weights, last)
    (last_there,) = gate((last_there,), (total_here,))
    theirs = finish(1, plan_here, mask, total, next_tokens, last_there, diag, gain_pair, next_weights)
    here = finish(0, plan_here, mask, total_here, next_tokens, last, diag, gain_pair, others=(theirs,))
    there = swap(theirs, CORE)
    return jnp.where(
        core == 0,
        jnp.concatenate([here, there], axis=1),
        jnp.concatenate([there, here], axis=1),
    )


def solution(mesh):
    eight_by_four = dict(mesh.shape) == {"dp": 8, "tensor": 4}
    return jax.shard_map(
        per_device_8x4 if eight_by_four else per_device,
        mesh=mesh,
        in_specs=(
            P("dp", "tensor"),
            P("dp", None, None),
            P(),
            P("dp", "tensor"),
            P("dp", "tensor"),
            P("dp", "tensor"),
            P(),
            P(),
        ),
        out_specs=P("dp", "tensor"),
        check_vma=False,
    )
```
